256 devices in a mesh: ctx: 32 (over z, x), chan: 4 (over y), section: 2 (over core).
Axes of the slice: x: 4, y: 4, z: 8, core: 2. Of those that a mesh axis runs over, the one named last changes fastest.
Arguments:
- signal: bfloat16 [16384, 4096], P(('section', 'ctx'), 'chan'), parts along dimension 0, may hold values from -60 to 60
- gating: bfloat16 [16384, 4096], P(('section', 'ctx'), 'chan'), parts along dimension 0, may hold values from -6 to 6
- filters: float32 [16384, 4096], P(('section', 'ctx'), 'chan'), parts along dimension 0, may hold values from -2 to 2
- skip_gain: float32 [8192], P(('section', 'chan')), parts along dimension 0, may hold values from 0.5 to 1.5
Outputs:
- output: bfloat16 [16384, 4096], P(('section', 'ctx'), 'chan'), parts along dimension 0
- cosine: float32 [16384], P(('section', 'ctx')), parts along dimension 0
The draws below stay inside these ranges and needn't reach their ends.
There are 2 independent parts, one for each index of `section`. The reference program is written for one: setup_inputs(seed, part) draws one part's arguments, and reference() takes and returns one part's arrays. A program takes and returns all parts, laid end to end along the dimension named above; each array names one. Nothing has to cross between parts.
All inputs are finite; a program needn't handle non-finite values.
Results may differ from the reference program's by a relative error of at most 0.011.
Values may be sent and summed in bfloat16 or wider, within the bound.
No kernel may reach another device: no remote copies, remote signals or barrier semaphores. Data moves between devices by JAX's collectives and lax.ppermute only.
A program may use at most 128 MiB of HBM per device.

```python
import math
import jax
import jax.numpy as jnp
from jax import lax

CHANNELS = 4096
SEQ_LEN = 8192


def draw_signal(key, part):
    key = jax.random.fold_in(key, 11)
    key_base, key_cols, key_rows = jax.random.split(key, 3)
    chan_pos = jnp.arange(CHANNELS, dtype=jnp.float32)
    col_scale = 10.0 ** ((chan_pos + jax.random.uniform(key_cols, (CHANNELS,))) / CHANNELS)
    base_vals = jnp.clip(jax.random.normal(key_base, (SEQ_LEN, CHANNELS)), -6.0, 6.0)
    row_scale = 10.0 ** jax.random.uniform(key_rows, (SEQ_LEN, 1))
    return (base_vals * row_scale * col_scale[None, :] * 0.1).astype(jnp.float32).astype(jnp.bfloat16)


def draw_filters(key, part):
    key = jax.random.fold_in(key, 23)
    key_base, key_rates = jax.random.split(key, 2)
    log_tau = jax.random.uniform(key_rates, (CHANNELS,), minval=math.log(30.0), maxval=math.log(4.0 * SEQ_LEN))
    base_vals = jnp.clip(jax.random.normal(key_base, (SEQ_LEN, CHANNELS)), -6.0, 6.0)
    tau_vals = jnp.exp(log_tau)[None, :]
    lag_pos = jnp.arange(SEQ_LEN, dtype=jnp.float32)[:, None]
    envelope = jnp.exp(-lag_pos / tau_vals) * jnp.sqrt(1.0 - jnp.exp(-2.0 / tau_vals))
    return (base_vals * envelope).astype(jnp.float32)


def levels(own_key, shape, pieces, low, largest):
    level = 1.0
    for position, parts in pieces:
        steps = jax.random.uniform(jax.random.fold_in(jax.random.fold_in(own_key, 6), position), (parts,), jnp.float32, low / len(pieces), largest / len(pieces))
        level = level * jnp.repeat(jnp.exp(steps), shape[position] // parts).reshape((-1,) + (1,) * (len(shape) - 1 - position))
    return level


def scatter_about(key, shape, scale, reach, shards=(), kind=jnp.bfloat16):
    gain = levels(key, shape, shards, -0.22, 0.18) if shards else 1.0
    array = jax.random.normal(key, shape, jnp.float32) * scale * gain
    return jnp.minimum(jnp.maximum(array, -reach), reach).astype(kind)


def setup_inputs(seed: int = 0, part: int = 0) -> dict:
    seeds = jax.random.split(jax.random.key(seed), 5)
    part_keys = jax.random.split(jax.random.fold_in(seeds[4], part), 5)
    signal = draw_signal(jax.random.fold_in(jax.random.fold_in(seeds[4], part), 71), part)
    gating = scatter_about(part_keys[1], (SEQ_LEN, CHANNELS), 1.0, 6.0, ((0, 32), (1, 4)))
    filters = draw_filters(jax.random.fold_in(jax.random.fold_in(seeds[4], part), 71), part)
    skip_gain = jnp.clip(0.5 + 1.0 * jax.random.uniform(part_keys[3], (CHANNELS,), jnp.float32) ** levels(part_keys[3], (CHANNELS,), ((0, 4),), -0.2, 0.2), 0.5, 1.5)
    return dict(signal=signal, gating=gating, filters=filters, skip_gain=skip_gain)


def causal_conv(sig_wide, fil_wide):
    seq_total, channel_count = sig_wide.shape
    block_size = math.gcd(channel_count, 256)
    block_count = channel_count // block_size
    sig_blocks = sig_wide.reshape(seq_total, block_count, block_size).transpose(1, 0, 2)
    fil_blocks = fil_wide.reshape(seq_total, block_count, block_size).transpose(1, 0, 2)

    def convolve(pair_parts):
        sig_part, fil_part = pair_parts
        padded = 2 * seq_total
        spectrum = jnp.fft.rfft(sig_part, n=padded, axis=0) * jnp.fft.rfft(fil_part, n=padded, axis=0)
        return jnp.fft.irfft(spectrum, n=padded, axis=0)[:seq_total]
    result_blocks = lax.map(convolve, (sig_blocks, fil_blocks))
    return result_blocks.transpose(1, 0, 2).reshape(seq_total, channel_count)

def reference(signal, gating, filters, skip_gain):
    signal_wide = signal.astype(jnp.float32)
    conv_out = causal_conv(signal_wide, filters.astype(jnp.float32)).astype(jnp.float32).astype(jnp.bfloat16)
    conv_out = lax.optimization_barrier(conv_out)
    mixed = gating.astype(jnp.float32) * (conv_out.astype(jnp.float32) + skip_gain[None, :] * signal_wide)
    output = mixed.astype(jnp.bfloat16)
    inner = lax.optimization_barrier(jnp.sum(signal_wide * mixed, axis=1))
    sig_sq = lax.optimization_barrier(jnp.sum(signal_wide * signal_wide, axis=1))
    out_sq = lax.optimization_barrier(jnp.sum(mixed * mixed, axis=1))
    cosine = inner / jnp.sqrt((sig_sq + 1e-06) * (out_sq + 1e-06))
    return (output, cosine)
```

```python
import math

import jax
import jax.numpy as jnp
import ml_dtypes
import numpy as np
from jax import lax
from jax.experimental import pallas as pl
from jax.experimental.pallas import tpu as pltpu
from jax.sharding import PartitionSpec as P

EPSILON = 1e-06
VMEM_LIMIT = 56 * 2**20
GROUP = 16


def conv_tables(blocks, span):
    total = blocks * span
    n1 = np.arange(blocks)
    n2 = np.arange(span)
    outer = 2 * np.pi * np.outer(4 * n1 + 1, n1) / (4 * blocks)
    twiddle = 2 * np.pi * np.outer(4 * n1 + 1, n2) / (4 * total)
    inner = 2 * np.pi * np.outer(n2, n2) / span
    eye = np.eye(GROUP)
    fwd_outer = np.concatenate([np.kron(np.cos(outer), eye), np.kron(-np.sin(outer), eye)], axis=0)
    inv_outer = np.concatenate(
        [np.kron(np.cos(outer.T), eye), np.kron(-np.sin(outer.T), eye)], axis=1
    )
    cos, sin = np.cos(inner), np.sin(inner)
    fwd_inner = np.block([[cos, -sin], [sin, cos]])
    inv_inner = np.block([[cos, sin], [-sin, cos]]) / total
    short = [t.astype(ml_dtypes.bfloat16) for t in (fwd_outer, inv_outer, fwd_inner, inv_inner)]
    wide = [np.cos(twiddle).astype(np.float32), np.sin(twiddle).astype(np.float32)]
    return short + wide


def dot(left, right):
    return jnp.dot(left, right, preferred_element_type=jnp.float32)


def prepare_kernel(sig_ref, fil_ref, out_ref, sq_ref):
    count, _, width, span = out_ref.shape
    sig = sig_ref[...]
    out_ref[:, 0] = sig.T.reshape(count, width, span)
    fil = fil_ref[...].astype(jnp.bfloat16)
    out_ref[:, 1] = fil.T.reshape(count, width, span)
    wide = sig.astype(jnp.float32)
    sq_ref[...] = token_sums(wide * wide)


def token_sums(terms):
    tokens, channels = terms.shape
    lanes = min(128, channels)
    part = terms[:, :lanes]
    for start in range(lanes, channels, lanes):
        part = part + terms[:, start : start + lanes]
    return jnp.sum(part.T, axis=0, keepdims=True)


def conv_kernel(in_ref, fo_ref, io_ref, fi_ref, ii_ref, cos_ref, sin_ref, out_ref):
    blocks, _, width, span = in_ref.shape
    rows = blocks * GROUP
    cos = jnp.broadcast_to(cos_ref[...][:, None, :], (blocks, GROUP, span)).reshape(rows, span)
    sin = jnp.broadcast_to(sin_ref[...][:, None, :], (blocks, GROUP, span)).reshape(rows, span)

    def spectrum(operand):
        outer = dot(fo_ref[...], operand)
        re, im = outer[:rows], outer[rows:]
        turned = jnp.concatenate([re * cos + im * sin, im * cos - re * sin], axis=1)
        both = dot(turned.astype(jnp.bfloat16), fi_ref[...])
        return both[:, :span], both[:, span:]

    for start in range(0, width, GROUP):
        sig = in_ref[:, 0, start : start + GROUP, :].reshape(rows, span)
        fil = in_ref[:, 1, start : start + GROUP, :].reshape(rows, span)
        sig_re, sig_im = spectrum(sig)
        fil_re, fil_im = spectrum(fil)
        prod = jnp.concatenate(
            [sig_re * fil_re - sig_im * fil_im, sig_re * fil_im + sig_im * fil_re], axis=1
        )
        back = dot(prod.astype(jnp.bfloat16), ii_ref[...])
        re, im = back[:, :span], back[:, span:]
        turned = jnp.concatenate([re * cos - im * sin, re * sin + im * cos], axis=0)
        conv = dot(io_ref[...], turned.astype(jnp.bfloat16))
        out_ref[:, start : start + GROUP, :] = conv.astype(jnp.bfloat16).reshape(blocks, GROUP, span)


def finish_kernel(conv_ref, sig_ref, gate_ref, skip_ref, out_ref, sums_ref):
    count, width, span = conv_ref.shape
    conv = conv_ref[...].reshape(count * width, span).T.astype(jnp.float32)
    sig = sig_ref[...].astype(jnp.float32)
    mixed = gate_ref[...].astype(jnp.float32) * (conv + skip_ref[...] * sig)
    out_ref[...] = mixed.astype(jnp.bfloat16)
    sums_ref[0:1] = token_sums(sig * mixed)
    sums_ref[1:2] = token_sums(mixed * mixed)


def call(kernel, out_shape, **kwargs):
    return pl.pallas_call(
        kernel,
        out_shape=out_shape,
        compiler_params=pltpu.CompilerParams(vmem_limit_bytes=VMEM_LIMIT),
        **kwargs,
    )


def local(signal, gating, filters, skip_gain):
    count = lax.axis_size("ctx")
    span, channels = signal.shape
    width = channels // count
    bf16, f32 = jnp.bfloat16, jnp.float32
    packed, sig_sq = call(
        prepare_kernel,
        (
            jax.ShapeDtypeStruct((count, 2, width, span), bf16),
            jax.ShapeDtypeStruct((1, span), f32),
        ),
    )(signal, filters)
    received = lax.all_to_all(packed, "ctx", split_axis=0, concat_axis=0, tiled=True)
    conv = call(conv_kernel, jax.ShapeDtypeStruct((count, width, span), bf16))(
        received, *conv_tables(count, span)
    )
    returned = lax.all_to_all(conv, "ctx", split_axis=0, concat_axis=0, tiled=True)
    result, sums = call(
        finish_kernel,
        (jax.ShapeDtypeStruct((span, channels), bf16), jax.ShapeDtypeStruct((2, span), f32)),
    )(returned, signal, gating, skip_gain.reshape(1, channels))
    sig_total = lax.psum(sig_sq[0], "chan")
    inner_total, out_total = lax.psum((sums[0], sums[1]), "chan")
    cosine = inner_total / jnp.sqrt((sig_total + EPSILON) * (out_total + EPSILON))
    return (result, cosine)


def solution(mesh):
    return jax.shard_map(
        local,
        mesh=mesh,
        in_specs=(
            P(("section", "ctx"), "chan"),
            P(("section", "ctx"), "chan"),
            P(("section", "ctx"), "chan"),
            P(("section", "chan")),
        ),
        out_specs=(P(("section", "ctx"), "chan"), P(("section", "ctx"))),
        check_vma=False,
    )
```

```python
import math

import jax
import jax.numpy as jnp
import ml_dtypes
import numpy as np
from jax import lax
from jax.experimental import pallas as pl
from jax.experimental.pallas import tpu as pltpu
from jax.sharding import PartitionSpec as P

EPSILON = 1e-06
VMEM_LIMIT = 20 * 2**20
GROUP = 16


def conv_tables(blocks, span):
    total = blocks * span
    n1 = np.arange(blocks)
    n2 = np.arange(span)
    outer = 2 * np.pi * np.outer(4 * n1 + 1, n1) / (4 * blocks)
    twiddle = 2 * np.pi * np.outer(4 * n1 + 1, n2) / (4 * total)
    inner = 2 * np.pi * np.outer(n2, n2) / span
    eye = np.eye(GROUP)
    fwd_outer = np.concatenate([np.kron(np.cos(outer), eye), np.kron(-np.sin(outer), eye)], axis=0)
    inv_outer = np.concatenate(
        [np.kron(np.cos(outer.T), eye), np.kron(-np.sin(outer.T), eye)], axis=1
    )
    cos, sin = np.cos(inner), np.sin(inner)
    fwd_inner = np.block([[cos, -sin], [sin, cos]])
    inv_inner = np.block([[cos, sin], [-sin, cos]]) / total
    short = [t.astype(ml_dtypes.bfloat16) for t in (fwd_outer, inv_outer, fwd_inner, inv_inner)]
    wide = [np.cos(twiddle).astype(np.float32), np.sin(twiddle).astype(np.float32)]
    return short + wide


def dot(left, right):
    return jnp.dot(left, right, preferred_element_type=jnp.float32)


def prepare_kernel(sig_ref, fil_ref, out_ref):
    count, _, width, span = out_ref.shape
    sig = sig_ref[...]
    out_ref[:, 0] = sig.T.reshape(count, width, span)
    fil = fil_ref[...].astype(jnp.bfloat16)
    out_ref[:, 1] = fil.T.reshape(count, width, span)


def token_sums(terms):
    tokens, channels = terms.shape
    lanes = min(128, channels)
    part = terms[:, :lanes]
    for start in range(lanes, channels, lanes):
        part = part + terms[:, start : start + lanes]
    return jnp.sum(part.T, axis=0, keepdims=True)


def conv_kernel(in_ref, fo_ref, io_ref, fi_ref, ii_ref, cos_ref, sin_ref, out_ref):
    blocks, _, width, span = in_ref.shape
    rows = blocks * GROUP
    cos = jnp.broadcast_to(cos_ref[...][:, None, :], (blocks, GROUP, span)).reshape(rows, span)
    sin = jnp.broadcast_to(sin_ref[...][:, None, :], (blocks, GROUP, span)).reshape(rows, span)

    def spectrum(operand):
        outer = dot(fo_ref[...], operand)
        re, im = outer[:rows], outer[rows:]
        turned = jnp.concatenate([re * cos + im * sin, im * cos - re * sin], axis=1)
        both = dot(turned.astype(jnp.bfloat16), fi_ref[...])
        return both[:, :span], both[:, span:]

    for start in range(0, width, GROUP):
        sig = in_ref[:, 0, start : start + GROUP, :].reshape(rows, span)
        fil = in_ref[:, 1, start : start + GROUP, :].reshape(rows, span)
        sig_re, sig_im = spectrum(sig)
        fil_re, fil_im = spectrum(fil)
        prod = jnp.concatenate(
            [sig_re * fil_re - sig_im * fil_im, sig_re * fil_im + sig_im * fil_re], axis=1
        )
        back = dot(prod.astype(jnp.bfloat16), ii_ref[...])
        re, im = back[:, :span], back[:, span:]
        turned = jnp.concatenate([re * cos - im * sin, re * sin + im * cos], axis=0)
        conv = dot(io_ref[...], turned.astype(jnp.bfloat16))
        out_ref[:, start : start + GROUP, :] = conv.astype(jnp.bfloat16).reshape(blocks, GROUP, span)


def finish_kernel(conv_ref, sig_ref, gate_ref, skip_ref, out_ref, sums_ref):
    count, width, span = conv_ref.shape
    conv = conv_ref[...].reshape(count * width, span).T.astype(jnp.float32)
    sig = sig_ref[...].astype(jnp.float32)
    mixed = gate_ref[...].astype(jnp.float32) * (conv + skip_ref[...] * sig)
    out_ref[...] = mixed.astype(jnp.bfloat16)
    sums_ref[0:1] = token_sums(sig * mixed)
    sums_ref[1:2] = token_sums(sig * sig)
    sums_ref[2:3] = token_sums(mixed * mixed)


def call(kernel, out_shape, **kwargs):
    return pl.pallas_call(
        kernel,
        out_shape=out_shape,
        compiler_params=pltpu.CompilerParams(vmem_limit_bytes=VMEM_LIMIT),
        **kwargs,
    )


def local(signal, gating, filters, skip_gain):
    count = lax.axis_size("ctx")
    span, channels = signal.shape
    width = channels // count
    bf16, f32 = jnp.bfloat16, jnp.float32
    packed = call(
        prepare_kernel, jax.ShapeDtypeStruct((count, 2, width, span), bf16)
    )(signal, filters)
    received = lax.all_to_all(packed, "ctx", split_axis=0, concat_axis=0, tiled=True)
    conv = call(conv_kernel, jax.ShapeDtypeStruct((count, width, span), bf16))(
        received, *conv_tables(count, span)
    )
    returned = lax.all_to_all(conv, "ctx", split_axis=0, concat_axis=0, tiled=True)
    result, sums = call(
        finish_kernel,
        (jax.ShapeDtypeStruct((span, channels), bf16), jax.ShapeDtypeStruct((3, span), f32)),
    )(returned, signal, gating, skip_gain.reshape(1, channels))
    parts = lax.axis_size("chan")
    others = [
        lax.ppermute(sums, "chan", [(i, (i + hop) % parts) for i in range(parts)])
        for hop in range(1, parts)
    ]
    inner_total, sig_total, out_total = sum(others, sums)
    cosine = inner_total / jnp.sqrt((sig_total + EPSILON) * (out_total + EPSILON))
    return (result, cosine)


def solution(mesh):
    return jax.shard_map(
        local,
        mesh=mesh,
        in_specs=(
            P(("section", "ctx"), "chan"),
            P(("section", "ctx"), "chan"),
            P(("section", "ctx"), "chan"),
            P(("section", "chan")),
        ),
        out_specs=(P(("section", "ctx"), "chan"), P(("section", "ctx"))),
        check_vma=False,
    )
```

```python
import math

import jax
import jax.numpy as jnp
import ml_dtypes
import numpy as np
from jax import lax
from jax.experimental import pallas as pl
from jax.experimental.pallas import tpu as pltpu
from jax.sharding import PartitionSpec as P

EPSILON = 1e-06
VMEM_LIMIT = 20 * 2**20
LANES = 128
GROUP = 8
TILES = 4


def conv_tables(blocks, span):
    total = blocks * span
    n1 = np.arange(blocks)
    n2 = np.arange(span)
    outer = 2 * np.pi * np.outer(4 * n1 + 1, n1) / (4 * blocks)
    twiddle = 2 * np.pi * np.outer(4 * n1 + 1, n2) / (4 * total)
    inner = 2 * np.pi * np.outer(n2, n2) / span
    eye = np.eye(GROUP)
    fwd_outer = np.concatenate([np.kron(np.cos(outer), eye), np.kron(-np.sin(outer), eye)], axis=0)
    inv_outer = np.concatenate(
        [np.kron(np.cos(outer.T), eye), np.kron(-np.sin(outer.T), eye)], axis=1
    )
    cos, sin = np.cos(inner), np.sin(inner)
    fwd_inner = np.block([[cos, -sin], [sin, cos]])
    inv_inner = np.block([[cos, sin], [-sin, cos]]) / total
    short = [t.astype(ml_dtypes.bfloat16) for t in (fwd_outer, inv_outer, fwd_inner, inv_inner)]
    wide = [np.cos(twiddle).astype(np.float32), np.sin(twiddle).astype(np.float32)]
    return short + wide


def dot(left, right):
    return jnp.dot(left, right, preferred_element_type=jnp.float32)


def tile_copies(hbm_ref, buf_ref, sem_ref):
    width = hbm_ref.shape[1] // TILES
    spans = [pl.ds(tile * width, width) for tile in range(TILES)]
    return [
        pltpu.make_async_copy(hbm_ref.at[:, span], buf_ref.at[:, span], sem_ref.at[tile])
        for tile, span in enumerate(spans)
    ]


def prepare_kernel(sig_ref, fil_ref, out_ref):
    devices, _, groups, rows, lanes = out_ref.shape
    parts = rows // GROUP
    span, channels = sig_ref.shape
    width, some = channels // TILES, devices // TILES
    for tile in range(TILES):
        for array, ref in enumerate((sig_ref, fil_ref)):
            block = ref[:, tile * width : (tile + 1) * width].astype(jnp.float32)
            turned = block.T.reshape(width // GROUP, GROUP, span)
            turned = jnp.concatenate(
                [turned[:, :, part * lanes : (part + 1) * lanes] for part in range(parts)], axis=1
            )
            out_ref[tile * some : (tile + 1) * some, array] = turned.astype(jnp.bfloat16).reshape(
                some, groups, rows, lanes
            )


def conv_kernel(in_ref, fo_ref, io_ref, fi_ref, ii_ref, cos_ref, sin_ref, out_ref):
    devices, _, groups, rows, lanes = in_ref.shape
    blocks = devices * rows // GROUP
    size = blocks * GROUP

    def turn(re, im, sign):
        cos, sin = (
            jnp.broadcast_to(ref[...][:, None, :], (blocks, GROUP, lanes)).reshape(size, lanes)
            for ref in (cos_ref, sin_ref)
        )
        if sign > 0:
            return re * cos - im * sin, re * sin + im * cos
        return re * cos + im * sin, im * cos - re * sin

    def spectrum(outer):
        turned = jnp.concatenate(turn(outer[:size], outer[size:], -1), axis=1)
        both = dot(turned.astype(jnp.bfloat16), fi_ref[...])
        return both[:, :lanes], both[:, lanes:]

    def product(group):
        pair = [in_ref[:, array, group].reshape(size, lanes) for array in range(2)]
        outer = dot(fo_ref[...], jnp.concatenate(pair, axis=1))
        sig_re, sig_im = spectrum(outer[:, :lanes])
        fil_re, fil_im = spectrum(outer[:, lanes:])
        prod = jnp.concatenate(
            [sig_re * fil_re - sig_im * fil_im, sig_re * fil_im + sig_im * fil_re], axis=1
        )
        back = dot(prod.astype(jnp.bfloat16), ii_ref[...])
        return jnp.concatenate(turn(back[:, :lanes], back[:, lanes:], 1), axis=0).astype(jnp.bfloat16)

    for group in range(0, groups, 2):
        pair = jnp.concatenate([product(group), product(group + 1)], axis=1)
        conv = dot(io_ref[...], pair).astype(jnp.bfloat16)
        for half in range(2):
            out_ref[:, group + half] = conv[:, half * lanes : (half + 1) * lanes].reshape(
                devices, rows, lanes
            )


def token_sums(terms):
    tokens, channels = terms.shape
    part = terms[:, :LANES]
    for start in range(LANES, channels, LANES):
        part = part + terms[:, start : start + LANES]
    return part


def finish_kernel(conv_ref, sig_ref, gate_ref, skip_ref, out_ref, sums_ref, out_buf, out_sem):
    devices, groups, rows, lanes = conv_ref.shape
    parts = rows // GROUP
    span, channels = out_buf.shape
    width, some = channels // TILES, devices // TILES
    copies = tile_copies(out_buf, out_ref, out_sem)
    sums = None
    for tile in range(TILES):
        turned = conv_ref[tile * some : (tile + 1) * some].astype(jnp.float32)
        turned = turned.reshape(some * groups, rows, lanes)
        conv = jnp.concatenate(
            [
                turned[:, part * GROUP : (part + 1) * GROUP].reshape(width, lanes).T
                for part in range(parts)
            ],
            axis=0,
        )
        at = slice(tile * width, (tile + 1) * width)
        sig = sig_ref[:, at].astype(jnp.float32)
        mixed = gate_ref[:, at].astype(jnp.float32) * (conv + skip_ref[:, at] * sig)
        out_buf[:, at] = mixed.astype(jnp.bfloat16)
        copies[tile].start()
        terms = [token_sums(sig * mixed), token_sums(sig * sig), token_sums(mixed * mixed)]
        sums = terms if sums is None else [a + b for a, b in zip(sums, terms)]
    for row, total in enumerate(sums):
        sums_ref[row : row + 1] = jnp.sum(total.T, axis=0, keepdims=True)
    for copy in copies:
        copy.wait()


def call(kernel, out_shape, **kwargs):
    return pl.pallas_call(
        kernel,
        out_shape=out_shape,
        compiler_params=pltpu.CompilerParams(vmem_limit_bytes=VMEM_LIMIT),
        **kwargs,
    )


def local(signal, gating, filters, skip_gain):
    count = lax.axis_size("ctx")
    span, channels = signal.shape
    width = channels // count
    parts = span // LANES
    packed_tail = (width // GROUP, parts * GROUP, LANES)
    bf16, f32 = jnp.bfloat16, jnp.float32
    hbm = pl.BlockSpec(memory_space=pltpu.HBM)
    vmem = pl.BlockSpec(memory_space=pltpu.VMEM)
    tile_sems = pltpu.SemaphoreType.DMA((TILES,))
    packed = call(
        prepare_kernel,
        jax.ShapeDtypeStruct((count, 2) + packed_tail, bf16),
        in_specs=[vmem, vmem],
        out_specs=vmem,
    )(signal, filters.astype(bf16))
    received = lax.all_to_all(packed, "ctx", split_axis=0, concat_axis=0, tiled=True)
    conv = call(conv_kernel, jax.ShapeDtypeStruct((count,) + packed_tail, bf16))(
        received, *conv_tables(count * parts, LANES)
    )
    returned = lax.all_to_all(conv, "ctx", split_axis=0, concat_axis=0, tiled=True)
    result, sums = call(
        finish_kernel,
        (jax.ShapeDtypeStruct((span, channels), bf16), jax.ShapeDtypeStruct((3, span), f32)),
        in_specs=[vmem] * 4,
        out_specs=(hbm, vmem),
        scratch_shapes=[pltpu.VMEM((span, channels), bf16), tile_sems],
    )(returned, signal, gating, skip_gain.reshape(1, channels))
    chans = lax.axis_size("chan")
    others = [
        lax.ppermute(sums, "chan", [(i, (i + hop) % chans) for i in range(chans)])
        for hop in range(1, chans)
    ]
    inner_total, sig_total, out_total = sum(others, sums)
    cosine = inner_total / jnp.sqrt((sig_total + EPSILON) * (out_total + EPSILON))
    return (result, cosine)


def solution(mesh):
    return jax.shard_map(
        local,
        mesh=mesh,
        in_specs=(
            P(("section", "ctx"), "chan"),
            P(("section", "ctx"), "chan"),
            P(("section", "ctx"), "chan"),
            P(("section", "chan")),
        ),
        out_specs=(P(("section", "ctx"), "chan"), P(("section", "ctx"))),
        check_vma=False,
    )
```

```python
import math

import jax
import jax.numpy as jnp
import ml_dtypes
import numpy as np
from jax import lax
from jax.experimental import pallas as pl
from jax.experimental.pallas import tpu as pltpu
from jax.sharding import PartitionSpec as P

EPSILON = 1e-06
VMEM_LIMIT = 20 * 2**20
LANES = 128
GROUP = 8
TILES = 4


def conv_tables(blocks, span):
    total = blocks * span
    n1 = np.arange(blocks)
    n2 = np.arange(span)
    outer = 2 * np.pi * np.outer(4 * n1 + 1, n1) / (4 * blocks)
    twiddle = 2 * np.pi * np.outer(4 * n1 + 1, n2) / (4 * total)
    inner = 2 * np.pi * np.outer(n2, n2) / span
    eye = np.eye(GROUP)
    fwd_outer = np.concatenate([np.kron(np.cos(outer), eye), np.kron(-np.sin(outer), eye)], axis=0)
    inv_outer = np.concatenate(
        [np.kron(np.cos(outer.T), eye), np.kron(-np.sin(outer.T), eye)], axis=1
    )
    cos, sin = np.cos(inner), np.sin(inner)
    fwd_inner = np.block([[cos, -sin], [sin, cos]])
    inv_inner = np.block([[cos, sin], [-sin, cos]]) / total
    short = [t.astype(ml_dtypes.bfloat16) for t in (fwd_outer, inv_outer, fwd_inner, inv_inner)]
    wide = [np.cos(twiddle).astype(np.float32), np.sin(twiddle).astype(np.float32)]
    return short + wide


def dot(left, right):
    return jnp.dot(left, right, preferred_element_type=jnp.float32)


def tile_copies(hbm_ref, buf_ref, sem_ref):
    width = hbm_ref.shape[1] // TILES
    spans = [pl.ds(tile * width, width) for tile in range(TILES)]
    return [
        pltpu.make_async_copy(hbm_ref.at[:, span], buf_ref.at[:, span], sem_ref.at[tile])
        for tile, span in enumerate(spans)
    ]


def prepare_kernel(sig_ref, fil_ref, out_ref, sq_ref):
    devices, _, groups, rows, lanes = out_ref.shape
    parts = rows // GROUP
    span, channels = sig_ref.shape
    width, some = channels // TILES, devices // TILES
    squares = None
    for tile in range(TILES):
        for array, ref in enumerate((sig_ref, fil_ref)):
            block = ref[:, tile * width : (tile + 1) * width].astype(jnp.float32)
            if array == 0:
                part = token_sums(block * block)
                squares = part if squares is None else squares + part
            turned = block.T.reshape(width // GROUP, GROUP, span)
            turned = jnp.concatenate(
                [turned[:, :, part * lanes : (part + 1) * lanes] for part in range(parts)], axis=1
            )
            out_ref[tile * some : (tile + 1) * some, array] = turned.astype(jnp.bfloat16).reshape(
                some, groups, rows, lanes
            )
    sq_ref[...] = jnp.sum(squares.T, axis=0, keepdims=True)


def conv_kernel(in_ref, fo_ref, io_ref, fi_ref, ii_ref, cos_ref, sin_ref, out_ref):
    devices, _, groups, rows, lanes = in_ref.shape
    blocks = devices * rows // GROUP
    size = blocks * GROUP

    def turn(re, im, sign):
        cos, sin = (
            jnp.broadcast_to(ref[...][:, None, :], (blocks, GROUP, lanes)).reshape(size, lanes)
            for ref in (cos_ref, sin_ref)
        )
        if sign > 0:
            return re * cos - im * sin, re * sin + im * cos
        return re * cos + im * sin, im * cos - re * sin

    def spectrum(outer):
        turned = jnp.concatenate(turn(outer[:size], outer[size:], -1), axis=1)
        both = dot(turned.astype(jnp.bfloat16), fi_ref[...])
        return both[:, :lanes], both[:, lanes:]

    def product(group):
        pair = [in_ref[:, array, group].reshape(size, lanes) for array in range(2)]
        outer = dot(fo_ref[...], jnp.concatenate(pair, axis=1))
        sig_re, sig_im = spectrum(outer[:, :lanes])
        fil_re, fil_im = spectrum(outer[:, lanes:])
        prod = jnp.concatenate(
            [sig_re * fil_re - sig_im * fil_im, sig_re * fil_im + sig_im * fil_re], axis=1
        )
        back = dot(prod.astype(jnp.bfloat16), ii_ref[...])
        return jnp.concatenate(turn(back[:, :lanes], back[:, lanes:], 1), axis=0).astype(jnp.bfloat16)

    for group in range(0, groups, 2):
        pair = jnp.concatenate([product(group), product(group + 1)], axis=1)
        conv = dot(io_ref[...], pair).astype(jnp.bfloat16)
        for half in range(2):
            out_ref[:, group + half] = conv[:, half * lanes : (half + 1) * lanes].reshape(
                devices, rows, lanes
            )


def token_sums(terms):
    tokens, channels = terms.shape
    part = terms[:, :LANES]
    for start in range(LANES, channels, LANES):
        part = part + terms[:, start : start + LANES]
    return part


def finish_kernel(conv_ref, sig_ref, gate_ref, skip_ref, out_ref, sums_ref, out_buf, out_sem):
    devices, groups, rows, lanes = conv_ref.shape
    parts = rows // GROUP
    span, channels = out_buf.shape
    width, some = channels // TILES, devices // TILES
    copies = tile_copies(out_buf, out_ref, out_sem)
    sums = None
    for tile in range(TILES):
        turned = conv_ref[tile * some : (tile + 1) * some].astype(jnp.float32)
        turned = turned.reshape(some * groups, rows, lanes)
        conv = jnp.concatenate(
            [
                turned[:, part * GROUP : (part + 1) * GROUP].reshape(width, lanes).T
                for part in range(parts)
            ],
            axis=0,
        )
        at = slice(tile * width, (tile + 1) * width)
        sig = sig_ref[:, at].astype(jnp.float32)
        mixed = gate_ref[:, at].astype(jnp.float32) * (conv + skip_ref[:, at] * sig)
        out_buf[:, at] = mixed.astype(jnp.bfloat16)
        copies[tile].start()
        terms = [token_sums(sig * mixed), token_sums(sig * sig), token_sums(mixed * mixed)]
        sums = terms if sums is None else [a + b for a, b in zip(sums, terms)]
    for row, total in enumerate(sums):
        sums_ref[row : row + 1] = jnp.sum(total.T, axis=0, keepdims=True)
    for copy in copies:
        copy.wait()


def call(kernel, out_shape, **kwargs):
    return pl.pallas_call(
        kernel,
        out_shape=out_shape,
        compiler_params=pltpu.CompilerParams(vmem_limit_bytes=VMEM_LIMIT),
        **kwargs,
    )


def local(signal, gating, filters, skip_gain):
    count = lax.axis_size("ctx")
    span, channels = signal.shape
    width = channels // count
    parts = span // LANES
    packed_tail = (width // GROUP, parts * GROUP, LANES)
    bf16, f32 = jnp.bfloat16, jnp.float32
    hbm = pl.BlockSpec(memory_space=pltpu.HBM)
    vmem = pl.BlockSpec(memory_space=pltpu.VMEM)
    tile_sems = pltpu.SemaphoreType.DMA((TILES,))
    packed, sig_sq = call(
        prepare_kernel,
        (
            jax.ShapeDtypeStruct((count, 2) + packed_tail, bf16),
            jax.ShapeDtypeStruct((1, span), f32),
        ),
        in_specs=[vmem, vmem],
        out_specs=(vmem, vmem),
    )(signal, filters.astype(bf16))
    chans, sections = lax.axis_size("chan"), lax.axis_size("section")
    last = sections - 1

    def total_first(part):
        total = part
        for hop in range(1, chans):
            total = total + lax.ppermute(
                part,
                ("chan", "section"),
                [(i * sections + last, (i + hop) % chans * sections + last) for i in range(chans)],
            )
        return total

    is_last = lax.axis_index("section") == last
    sig_sq = lax.cond(is_last, total_first, lambda part: part, sig_sq)
    packed, sig_sq = lax.optimization_barrier((packed, sig_sq))
    received = lax.all_to_all(packed, "ctx", split_axis=0, concat_axis=0, tiled=True)
    conv = call(conv_kernel, jax.ShapeDtypeStruct((count,) + packed_tail, bf16))(
        received, *conv_tables(count * parts, LANES)
    )
    returned = lax.all_to_all(conv, "ctx", split_axis=0, concat_axis=0, tiled=True)
    result, sums = call(
        finish_kernel,
        (jax.ShapeDtypeStruct((span, channels), bf16), jax.ShapeDtypeStruct((3, span), f32)),
        in_specs=[vmem] * 4,
        out_specs=(hbm, vmem),
        scratch_shapes=[pltpu.VMEM((span, channels), bf16), tile_sems],
    )(returned, signal, gating, skip_gain.reshape(1, channels))
    others = [
        lax.ppermute(sums, "chan", [(i, (i + hop) % chans) for i in range(chans)])
        for hop in range(1, chans)
    ]
    inner_total, sig_total, out_total = sum(others, sums)
    sig_total = jnp.where(is_last, sig_sq[0], sig_total)
    cosine = inner_total / jnp.sqrt((sig_total + EPSILON) * (out_total + EPSILON))
    return (result, cosine)


def solution(mesh):
    return jax.shard_map(
        local,
        mesh=mesh,
        in_specs=(
            P(("section", "ctx"), "chan"),
            P(("section", "ctx"), "chan"),
            P(("section", "ctx"), "chan"),
            P(("section", "chan")),
        ),
        out_specs=(P(("section", "ctx"), "chan"), P(("section", "ctx"))),
        check_vma=False,
    )
```

```python
import math

import jax
import jax.numpy as jnp
import ml_dtypes
import numpy as np
from jax import lax
from jax.experimental import pallas as pl
from jax.experimental.pallas import tpu as pltpu
from jax.sharding import PartitionSpec as P

EPSILON = 1e-06
VMEM_LIMIT = 20 * 2**20
LANES = 128
GROUP = 8
TILES = 4
RADIX = 4
COS, SIN, HALF = math.cos(math.pi / 8), math.sin(math.pi / 8), math.sqrt(0.5)


def conv_tables(blocks, span):
    total = blocks * span
    few = blocks // RADIX
    m, r = np.arange(few), np.arange(span)
    k1 = RADIX * np.arange(few)[None, :] + np.arange(RADIX)[:, None]
    outer = 2 * np.pi * (4 * k1 + 1)[:, :, None] * m / (4 * blocks)
    twiddle = 2 * np.pi * (4 * k1 + 1).reshape(-1, 1) * r / (4 * total)
    inner = 2 * np.pi * np.outer(r, r) / span

    def split(cos, sin):
        return np.block([[cos, -sin], [sin, cos]])

    def spread(angles):
        eye = np.eye(GROUP)
        return split(np.kron(np.cos(angles), eye), np.kron(np.sin(angles), eye))

    fwd_outer = np.stack([spread(-angles) for angles in outer])
    inv_outer = np.stack([spread(angles.T) for angles in outer])
    fwd_inner = split(np.cos(inner), np.sin(inner))
    inv_inner = split(np.cos(inner), -np.sin(inner)) / total
    short = [t.astype(ml_dtypes.bfloat16) for t in (fwd_outer, inv_outer, fwd_inner, inv_inner)]
    wide = [np.cos(twiddle).astype(np.float32), np.sin(twiddle).astype(np.float32)]
    return short + wide


def quarters(x0, x1, x2, x3):
    even, odd = HALF * x2, (COS * x1, SIN * x1, COS * x3, SIN * x3)
    plus, minus = x0 + even, x0 - even
    c, d = odd[0] + odd[3], odd[1] - odd[2]
    e, f = odd[1] + odd[2], odd[0] - odd[3]
    return [
        (plus + c, -(e + even)),
        (minus - d, even - f),
        (plus - c, e - even),
        (minus + d, f + even),
    ]


def recombined(parts):
    (r0, i0), (r1, i1), (r2, i2), (r3, i3) = parts
    a, b, c, d = r0 - r2, r1 - r3, i0 - i2, i1 - i3
    e, f = r0 + r2, r1 + r3
    return [
        e + f,
        COS * (a - d) - SIN * (b + c),
        HALF * ((e - f) - ((i0 + i2) - (i1 + i3))),
        SIN * (a + d) + COS * (b - c),
    ]


def dot(left, right):
    return jnp.dot(left, right, preferred_element_type=jnp.float32)


def tile_copies(hbm_ref, buf_ref, sem_ref):
    width = hbm_ref.shape[1] // TILES
    spans = [pl.ds(tile * width, width) for tile in range(TILES)]
    return [
        pltpu.make_async_copy(hbm_ref.at[:, span], buf_ref.at[:, span], sem_ref.at[tile])
        for tile, span in enumerate(spans)
    ]


def prepare_kernel(sig_ref, fil_ref, out_ref, sq_ref):
    devices, _, groups, rows, lanes = out_ref.shape
    parts = rows // GROUP
    span, channels = sig_ref.shape
    width, some = channels // TILES, devices // TILES
    squares = None
    for tile in range(TILES):
        for array, ref in enumerate((sig_ref, fil_ref)):
            block = ref[:, tile * width : (tile + 1) * width].astype(jnp.float32)
            if array == 0:
                part = token_sums(block * block)
                squares = part if squares is None else squares + part
            turned = block.T.reshape(width // GROUP, GROUP, span)
            turned = jnp.concatenate(
                [turned[:, :, part * lanes : (part + 1) * lanes] for part in range(parts)], axis=1
            )
            out_ref[tile * some : (tile + 1) * some, array] = turned.astype(jnp.bfloat16).reshape(
                some, groups, rows, lanes
            )
    sq_ref[...] = jnp.sum(squares.T, axis=0, keepdims=True)


def conv_kernel(in_ref, fo_ref, io_ref, fi_ref, ii_ref, cos_ref, sin_ref, out_ref):
    devices, _, groups, rows, lanes = in_ref.shape
    some = devices // RADIX
    size = some * rows
    few = size // GROUP

    def turn(re, im, j, sign):
        cos, sin = (
            jnp.broadcast_to(
                ref[j * few : (j + 1) * few][:, None, :], (few, GROUP, lanes)
            ).reshape(size, lanes)
            for ref in (cos_ref, sin_ref)
        )
        if sign > 0:
            return re * cos - im * sin, re * sin + im * cos
        return re * cos + im * sin, im * cos - re * sin

    def outer(group):
        blocks = []
        for q in range(RADIX):
            pair = [
                in_ref[q * some : (q + 1) * some, array, group].reshape(size, lanes)
                for array in range(2)
            ]
            blocks.append(jnp.concatenate(pair, axis=1).astype(jnp.float32))
        return [
            dot(fo_ref[j], jnp.concatenate([re, im], axis=0).astype(jnp.bfloat16))
            for j, (re, im) in enumerate(quarters(*blocks))
        ]

    def spectra(outers):
        turned = []
        for j, part in enumerate(outers):
            turned.append(
                [
                    jnp.concatenate(
                        turn(part[:size, at : at + lanes], part[size:, at : at + lanes], j, -1), axis=1
                    ).astype(jnp.bfloat16)
                    for at in (0, lanes)
                ]
            )
        return [dot(jnp.concatenate(part, axis=0), fi_ref[...]) for part in zip(*turned)]

    def product(sig, fil):
        sig_re, sig_im = sig[:, :lanes], sig[:, lanes:]
        fil_re, fil_im = fil[:, :lanes], fil[:, lanes:]
        prod = jnp.concatenate(
            [sig_re * fil_re - sig_im * fil_im, sig_re * fil_im + sig_im * fil_re], axis=1
        )
        return dot(prod.astype(jnp.bfloat16), ii_ref[...])

    def unturned(spread):
        results = []
        for j in range(RADIX):
            back = spread[j * size : (j + 1) * size]
            back = turn(back[:, :lanes], back[:, lanes:], j, 1)
            results.append(jnp.concatenate(back, axis=0).astype(jnp.bfloat16))
        return results

    def finish(group, first, second):
        parts = []
        for j, pair in enumerate(zip(first, second)):
            part = dot(io_ref[j], jnp.concatenate(pair, axis=1))
            parts.append((part[:size], part[size:]))
        for q, conv in enumerate(recombined(parts)):
            conv = conv.astype(jnp.bfloat16)
            for half in range(2):
                out_ref[q * some : (q + 1) * some, group + half] = conv[
                    :, half * lanes : (half + 1) * lanes
                ].reshape(some, rows, lanes)

    outers = [outer(group) for group in range(groups)]
    specs = [spectra(part) for part in outers]
    spreads = [product(*spec) for spec in specs]
    results = [unturned(spread) for spread in spreads]
    for group in range(0, groups, 2):
        finish(group, results[group], results[group + 1])


def token_sums(terms):
    tokens, channels = terms.shape
    part = terms[:, :LANES]
    for start in range(LANES, channels, LANES):
        part = part + terms[:, start : start + LANES]
    return part


def finish_kernel(conv_ref, sig_ref, gate_ref, skip_ref, out_ref, sums_ref):
    devices, groups, rows, lanes = conv_ref.shape
    parts = rows // GROUP
    span, channels = out_ref.shape
    width, some = channels // TILES, devices // TILES
    sums = None
    for tile in range(TILES):
        turned = conv_ref[tile * some : (tile + 1) * some].astype(jnp.float32)
        turned = turned.reshape(some * groups, rows, lanes)
        conv = jnp.concatenate(
            [
                turned[:, part * GROUP : (part + 1) * GROUP].reshape(width, lanes).T
                for part in range(parts)
            ],
            axis=0,
        )
        at = slice(tile * width, (tile + 1) * width)
        sig = sig_ref[:, at].astype(jnp.float32)
        mixed = gate_ref[:, at].astype(jnp.float32) * (conv + skip_ref[:, at] * sig)
        out_ref[:, at] = mixed.astype(jnp.bfloat16)
        terms = [token_sums(sig * mixed), token_sums(sig * sig), token_sums(mixed * mixed)]
        sums = terms if sums is None else [a + b for a, b in zip(sums, terms)]
    for row, total in enumerate(sums):
        sums_ref[row : row + 1] = jnp.sum(total.T, axis=0, keepdims=True)


def deliver_kernel(in_ref, out_ref, sem_ref):
    copies = tile_copies(in_ref, out_ref, sem_ref)
    for copy in copies:
        copy.start()
    for copy in copies:
        copy.wait()


def call(kernel, out_shape, **kwargs):
    return pl.pallas_call(
        kernel,
        out_shape=out_shape,
        compiler_params=pltpu.CompilerParams(vmem_limit_bytes=VMEM_LIMIT),
        **kwargs,
    )


def local(signal, gating, filters, skip_gain):
    count = lax.axis_size("ctx")
    span, channels = signal.shape
    width = channels // count
    parts = span // LANES
    packed_tail = (width // GROUP, parts * GROUP, LANES)
    bf16, f32 = jnp.bfloat16, jnp.float32
    hbm = pl.BlockSpec(memory_space=pltpu.HBM)
    vmem = pl.BlockSpec(memory_space=pltpu.VMEM)
    tile_sems = pltpu.SemaphoreType.DMA((TILES,))
    packed, sig_sq = call(
        prepare_kernel,
        (
            jax.ShapeDtypeStruct((count, 2) + packed_tail, bf16),
            jax.ShapeDtypeStruct((1, span), f32),
        ),
        in_specs=[vmem, vmem],
        out_specs=(vmem, vmem),
    )(signal, filters.astype(bf16))
    chans, sections = lax.axis_size("chan"), lax.axis_size("section")
    last = sections - 1

    def total_first(part):
        total = part
        for hop in range(1, chans):
            total = total + lax.ppermute(
                part,
                ("chan", "section"),
                [(i * sections + last, (i + hop) % chans * sections + last) for i in range(chans)],
            )
        return total

    is_last = lax.axis_index("section") == last
    sig_sq = lax.cond(is_last, total_first, lambda part: part, sig_sq)
    packed, sig_sq = lax.optimization_barrier((packed, sig_sq))
    received = lax.all_to_all(packed, "ctx", split_axis=0, concat_axis=0, tiled=True)
    conv = call(conv_kernel, jax.ShapeDtypeStruct((count,) + packed_tail, bf16))(
        received, *conv_tables(count * parts, LANES)
    )
    returned = lax.all_to_all(conv, "ctx", split_axis=0, concat_axis=0, tiled=True)
    mixed, sums = call(
        finish_kernel,
        (jax.ShapeDtypeStruct((span, channels), bf16), jax.ShapeDtypeStruct((3, span), f32)),
        in_specs=[vmem] * 4,
        out_specs=(vmem, vmem),
    )(returned, signal, gating, skip_gain.reshape(1, channels))
    result = call(
        deliver_kernel,
        jax.ShapeDtypeStruct((span, channels), bf16),
        in_specs=[pl.BlockSpec(memory_space=pl.ANY)],
        out_specs=hbm,
        scratch_shapes=[tile_sems],
    )(mixed)
    others = [
        lax.ppermute(sums, "chan", [(i, (i + hop) % chans) for i in range(chans)])
        for hop in range(1, chans)
    ]
    inner_total, sig_total, out_total = sum(others, sums)
    sig_total = jnp.where(is_last, sig_sq[0], sig_total)
    cosine = inner_total / jnp.sqrt((sig_total + EPSILON) * (out_total + EPSILON))
    return (result, cosine)


def solution(mesh):
    return jax.shard_map(
        local,
        mesh=mesh,
        in_specs=(
            P(("section", "ctx"), "chan"),
            P(("section", "ctx"), "chan"),
            P(("section", "ctx"), "chan"),
            P(("section", "chan")),
        ),
        out_specs=(P(("section", "ctx"), "chan"), P(("section", "ctx"))),
        check_vma=False,
    )
```

```python
import math

import jax
import jax.numpy as jnp
import ml_dtypes
import numpy as np
from jax import lax
from jax.experimental import pallas as pl
from jax.experimental.pallas import tpu as pltpu
from jax.sharding import PartitionSpec as P

EPSILON = 1e-06
VMEM_LIMIT = 20 * 2**20
LANES = 128
GROUP = 8
TILES = 4
RADIX = 4
COS, SIN, HALF = math.cos(math.pi / 8), math.sin(math.pi / 8), math.sqrt(0.5)


def conv_tables(blocks, span):
    total = blocks * span
    few = blocks // RADIX
    m, r = np.arange(few), np.arange(span)
    k1 = RADIX * np.arange(few)[None, :] + np.arange(RADIX)[:, None]
    outer = 2 * np.pi * (4 * k1 + 1)[:, :, None] * m / (4 * blocks)
    twiddle = 2 * np.pi * (4 * k1 + 1).reshape(-1, 1) * r / (4 * total)
    inner = 2 * np.pi * np.outer(r, r) / span

    def split(cos, sin):
        return np.block([[cos, -sin], [sin, cos]])

    def spread(angles):
        eye = np.eye(GROUP)
        return split(np.kron(np.cos(angles), eye), np.kron(np.sin(angles), eye))

    fwd_outer = np.stack([spread(-angles) for angles in outer])
    inv_outer = np.stack([spread(angles.T) for angles in outer])
    fwd_inner = split(np.cos(inner), np.sin(inner))
    inv_inner = split(np.cos(inner), -np.sin(inner)) / total
    short = [t.astype(ml_dtypes.bfloat16) for t in (fwd_outer, inv_outer, fwd_inner, inv_inner)]
    wide = [np.cos(twiddle).astype(np.float32), np.sin(twiddle).astype(np.float32)]
    return short + wide


def quarters(x0, x1, x2, x3):
    even, odd = HALF * x2, (COS * x1, SIN * x1, COS * x3, SIN * x3)
    plus, minus = x0 + even, x0 - even
    c, d = odd[0] + odd[3], odd[1] - odd[2]
    e, f = odd[1] + odd[2], odd[0] - odd[3]
    return [
        (plus + c, -(e + even)),
        (minus - d, even - f),
        (plus - c, e - even),
        (minus + d, f + even),
    ]


def recombined(parts):
    (r0, i0), (r1, i1), (r2, i2), (r3, i3) = parts
    a, b, c, d = r0 - r2, r1 - r3, i0 - i2, i1 - i3
    e, f = r0 + r2, r1 + r3
    return [
        e + f,
        COS * (a - d) - SIN * (b + c),
        HALF * ((e - f) - ((i0 + i2) - (i1 + i3))),
        SIN * (a + d) + COS * (b - c),
    ]


def dot(left, right):
    return jnp.dot(left, right, preferred_element_type=jnp.float32)


def tile_copies(hbm_ref, buf_ref, sem_ref):
    width = hbm_ref.shape[1] // TILES
    spans = [pl.ds(tile * width, width) for tile in range(TILES)]
    return [
        pltpu.make_async_copy(hbm_ref.at[:, span], buf_ref.at[:, span], sem_ref.at[tile])
        for tile, span in enumerate(spans)
    ]


def prepare_kernel(sig_ref, fil_ref, out_ref, sq_ref):
    devices, _, groups, rows, lanes = out_ref.shape
    parts = rows // GROUP
    span, channels = sig_ref.shape
    width, some = channels // TILES, devices // TILES
    squares = None
    for tile in range(TILES):
        for array, ref in enumerate((sig_ref, fil_ref)):
            block = ref[:, tile * width : (tile + 1) * width].astype(jnp.float32)
            if array == 0:
                part = token_sums(block * block)
                squares = part if squares is None else squares + part
            turned = block.T.reshape(width // GROUP, GROUP, span)
            turned = jnp.concatenate(
                [turned[:, :, part * lanes : (part + 1) * lanes] for part in range(parts)], axis=1
            )
            out_ref[tile * some : (tile + 1) * some, array] = turned.astype(jnp.bfloat16).reshape(
                some, groups, rows, lanes
            )
    sq_ref[...] = jnp.sum(squares.T, axis=0, keepdims=True)


def conv_kernel(in_ref, fo_ref, io_ref, fi_ref, ii_ref, cos_ref, sin_ref, out_ref):
    devices, _, groups, rows, lanes = in_ref.shape
    some = devices // RADIX
    size = some * rows
    few = size // GROUP

    def turn(re, im, j, sign):
        cos, sin = (
            jnp.broadcast_to(
                ref[j * few : (j + 1) * few][:, None, :], (few, GROUP, lanes)
            ).reshape(size, lanes)
            for ref in (cos_ref, sin_ref)
        )
        if sign > 0:
            return re * cos - im * sin, re * sin + im * cos
        return re * cos + im * sin, im * cos - re * sin

    def outer(group):
        blocks = []
        for q in range(RADIX):
            pair = [
                in_ref[q * some : (q + 1) * some, array, group].reshape(size, lanes)
                for array in range(2)
            ]
            blocks.append(jnp.concatenate(pair, axis=1).astype(jnp.float32))
        return [
            dot(fo_ref[j], jnp.concatenate([re, im], axis=0).astype(jnp.bfloat16))
            for j, (re, im) in enumerate(quarters(*blocks))
        ]

    def spectra(outers):
        turned = []
        for j, part in enumerate(outers):
            turned.append(
                [
                    jnp.concatenate(
                        turn(part[:size, at : at + lanes], part[size:, at : at + lanes], j, -1), axis=1
                    ).astype(jnp.bfloat16)
                    for at in (0, lanes)
                ]
            )
        return [dot(jnp.concatenate(part, axis=0), fi_ref[...]) for part in zip(*turned)]

    def product(sig, fil):
        sig_re, sig_im = sig[:, :lanes], sig[:, lanes:]
        fil_re, fil_im = fil[:, :lanes], fil[:, lanes:]
        prod = jnp.concatenate(
            [sig_re * fil_re - sig_im * fil_im, sig_re * fil_im + sig_im * fil_re], axis=1
        )
        return dot(prod.astype(jnp.bfloat16), ii_ref[...])

    def unturned(spread):
        results = []
        for j in range(RADIX):
            back = spread[j * size : (j + 1) * size]
            back = turn(back[:, :lanes], back[:, lanes:], j, 1)
            results.append(jnp.concatenate(back, axis=0).astype(jnp.bfloat16))
        return results

    def finish(group, first, second):
        parts = []
        for j, pair in enumerate(zip(first, second)):
            part = dot(io_ref[j], jnp.concatenate(pair, axis=1))
            parts.append((part[:size], part[size:]))
        for q, conv in enumerate(recombined(parts)):
            conv = conv.astype(jnp.bfloat16)
            for half in range(2):
                out_ref[q * some : (q + 1) * some, group + half] = conv[
                    :, half * lanes : (half + 1) * lanes
                ].reshape(some, rows, lanes)

    outers = [outer(group) for group in range(groups)]
    specs = [spectra(part) for part in outers]
    spreads = [product(*spec) for spec in specs]
    results = [unturned(spread) for spread in spreads]
    for group in range(0, groups, 2):
        finish(group, results[group], results[group + 1])


def token_sums(terms):
    tokens, channels = terms.shape
    part = terms[:, :LANES]
    for start in range(LANES, channels, LANES):
        part = part + terms[:, start : start + LANES]
    return part


def finish_kernel(conv_ref, sig_ref, gate_ref, skip_ref, out_ref, sums_ref):
    devices, groups, rows, lanes = conv_ref.shape
    parts = rows // GROUP
    span, channels = out_ref.shape
    width, some = channels // TILES, devices // TILES
    sums = None
    for tile in range(TILES):
        turned = conv_ref[tile * some : (tile + 1) * some].astype(jnp.float32)
        turned = turned.reshape(some * groups, rows, lanes)
        conv = jnp.concatenate(
            [
                turned[:, part * GROUP : (part + 1) * GROUP].reshape(width, lanes).T
                for part in range(parts)
            ],
            axis=0,
        )
        at = slice(tile * width, (tile + 1) * width)
        sig = sig_ref[:, at].astype(jnp.float32)
        mixed = gate_ref[:, at].astype(jnp.float32) * (conv + skip_ref[:, at] * sig)
        out_ref[:, at] = mixed.astype(jnp.bfloat16)
        terms = [token_sums(sig * mixed), token_sums(sig * sig), token_sums(mixed * mixed)]
        sums = terms if sums is None else [a + b for a, b in zip(sums, terms)]
    for row, total in enumerate(sums):
        sums_ref[row : row + 1] = jnp.sum(total.T, axis=0, keepdims=True)


def deliver_kernel(in_ref, out_ref, sem_ref):
    copies = tile_copies(in_ref, out_ref, sem_ref)
    for copy in copies:
        copy.start()
    for copy in copies:
        copy.wait()


def call(kernel, out_shape, **kwargs):
    return pl.pallas_call(
        kernel,
        out_shape=out_shape,
        compiler_params=pltpu.CompilerParams(vmem_limit_bytes=VMEM_LIMIT),
        **kwargs,
    )


def local(signal, gating, filters, skip_gain):
    count = lax.axis_size("ctx")
    span, channels = signal.shape
    width = channels // count
    parts = span // LANES
    packed_tail = (width // GROUP, parts * GROUP, LANES)
    bf16, f32 = jnp.bfloat16, jnp.float32
    hbm = pl.BlockSpec(memory_space=pltpu.HBM)
    vmem = pl.BlockSpec(memory_space=pltpu.VMEM)
    tile_sems = pltpu.SemaphoreType.DMA((TILES,))
    packed, sig_sq = call(
        prepare_kernel,
        (
            jax.ShapeDtypeStruct((count, 2) + packed_tail, bf16),
            jax.ShapeDtypeStruct((1, span), f32),
        ),
        in_specs=[vmem, vmem],
        out_specs=(vmem, vmem),
    )(signal, filters.astype(bf16))
    chans, sections = lax.axis_size("chan"), lax.axis_size("section")
    last = sections - 1

    def total_first(part):
        total = part
        for hop in range(1, chans):
            total = total + lax.ppermute(
                part,
                ("chan", "section"),
                [(i * sections + last, (i + hop) % chans * sections + last) for i in range(chans)],
            )
        return total

    is_last = lax.axis_index("section") == last
    sig_sq = lax.cond(is_last, total_first, lambda part: part, sig_sq)
    packed, sig_sq = lax.optimization_barrier((packed, sig_sq))
    received = lax.all_to_all(packed, "ctx", split_axis=0, concat_axis=0, tiled=True)
    conv = call(conv_kernel, jax.ShapeDtypeStruct((count,) + packed_tail, bf16))(
        received, *conv_tables(count * parts, LANES)
    )
    returned = lax.all_to_all(conv, "ctx", split_axis=0, concat_axis=0, tiled=True)
    mixed, sums = call(
        finish_kernel,
        (jax.ShapeDtypeStruct((span, channels), bf16), jax.ShapeDtypeStruct((3, span), f32)),
        in_specs=[vmem] * 4,
        out_specs=(vmem, vmem),
    )(returned, signal, gating, skip_gain.reshape(1, channels))
    result = call(
        deliver_kernel,
        jax.ShapeDtypeStruct((span, channels), bf16),
        in_specs=[pl.BlockSpec(memory_space=pl.ANY)],
        out_specs=hbm,
        scratch_shapes=[tile_sems],
    )(mixed)
    reach = 2
    while reach <= chans:
        sums = sums + lax.ppermute(sums, "chan", [(i, i ^ (reach - 1)) for i in range(chans)])
        reach *= 2
    inner_total, sig_total, out_total = sums
    sig_total = jnp.where(is_last, sig_sq[0], sig_total)
    cosine = inner_total / jnp.sqrt((sig_total + EPSILON) * (out_total + EPSILON))
    return (result, cosine)


def solution(mesh):
    return jax.shard_map(
        local,
        mesh=mesh,
        in_specs=(
            P(("section", "ctx"), "chan"),
            P(("section", "ctx"), "chan"),
            P(("section", "ctx"), "chan"),
            P(("section", "chan")),
        ),
        out_specs=(P(("section", "ctx"), "chan"), P(("section", "ctx"))),
        check_vma=False,
    )
```

```python
import math

import jax
import jax.numpy as jnp
import ml_dtypes
import numpy as np
from jax import lax
from jax.experimental import pallas as pl
from jax.experimental.pallas import tpu as pltpu
from jax.sharding import PartitionSpec as P

EPSILON = 1e-06
VMEM_LIMIT = 20 * 2**20
LANES = 128
GROUP = 8
TILES = 4
RADIX = 4
COS, SIN, HALF = math.cos(math.pi / 8), math.sin(math.pi / 8), math.sqrt(0.5)


def two_parts(table):
    high = table.astype(ml_dtypes.bfloat16)
    low = (table - high.astype(np.float64)).astype(ml_dtypes.bfloat16)
    return np.concatenate([high, low], axis=-1)


def mild_scale(table):
    scales = 1 + np.arange(1000) / 1000
    errors = [
        np.square((scale * table).astype(ml_dtypes.bfloat16).astype(np.float64) / scale - table).mean()
        for scale in scales
    ]
    return scales[int(np.argmin(errors))]


def conv_tables(blocks, span):
    total = blocks * span
    few = blocks // RADIX
    m, r = np.arange(few), np.arange(span)
    k1 = RADIX * np.arange(few)[None, :] + np.arange(RADIX)[:, None]
    outer = 2 * np.pi * (4 * k1 + 1)[:, :, None] * m / (4 * blocks)
    twiddle = 2 * np.pi * (4 * k1 + 1).reshape(-1, 1) * r / (4 * total)
    inner = 2 * np.pi * np.outer(r, r) / span

    def split(cos, sin):
        return np.block([[cos, -sin], [sin, cos]])

    def spread(angles):
        eye = np.eye(GROUP)
        return split(np.kron(np.cos(angles), eye), np.kron(np.sin(angles), eye))

    scale = mild_scale(np.cos(inner))
    fwd_outer = two_parts(np.stack([spread(-angles) for angles in outer]))
    inv_outer = two_parts(np.stack([spread(angles.T) for angles in outer]) / (total * scale**3))
    fwd_inner = (scale * split(np.cos(inner), np.sin(inner))).astype(ml_dtypes.bfloat16)
    inv_inner = (scale * split(np.cos(inner), -np.sin(inner))).astype(ml_dtypes.bfloat16)
    short = [fwd_outer, inv_outer, fwd_inner, inv_inner]
    wide = [np.cos(twiddle).astype(np.float32), np.sin(twiddle).astype(np.float32)]
    return short + wide


def quarters(x0, x1, x2, x3):
    even, odd = HALF * x2, (COS * x1, SIN * x1, COS * x3, SIN * x3)
    plus, minus = x0 + even, x0 - even
    c, d = odd[0] + odd[3], odd[1] - odd[2]
    e, f = odd[1] + odd[2], odd[0] - odd[3]
    return [
        (plus + c, -(e + even)),
        (minus - d, even - f),
        (plus - c, e - even),
        (minus + d, f + even),
    ]


def recombined(parts):
    (r0, i0), (r1, i1), (r2, i2), (r3, i3) = parts
    a, b, c, d = r0 - r2, r1 - r3, i0 - i2, i1 - i3
    e, f = r0 + r2, r1 + r3
    return [
        e + f,
        COS * (a - d) - SIN * (b + c),
        HALF * ((e - f) - ((i0 + i2) - (i1 + i3))),
        SIN * (a + d) + COS * (b - c),
    ]


def dot(left, right):
    return jnp.dot(left, right, preferred_element_type=jnp.float32)


def outer_dot(table, values):
    values = values.astype(jnp.bfloat16)
    return dot(table, jnp.concatenate([values, values], axis=0))


def tile_copies(hbm_ref, buf_ref, sem_ref):
    width = hbm_ref.shape[1] // TILES
    spans = [pl.ds(tile * width, width) for tile in range(TILES)]
    return [
        pltpu.make_async_copy(hbm_ref.at[:, span], buf_ref.at[:, span], sem_ref.at[tile])
        for tile, span in enumerate(spans)
    ]


def prepare_kernel(sig_ref, fil_ref, out_ref, sq_ref):
    devices, _, groups, rows, lanes = out_ref.shape
    parts = rows // GROUP
    span, channels = sig_ref.shape
    width, some = channels // TILES, devices // TILES
    squares = None
    for tile in range(TILES):
        for array, ref in enumerate((sig_ref, fil_ref)):
            block = ref[:, tile * width : (tile + 1) * width].astype(jnp.float32)
            if array == 0:
                part = token_sums(block * block)
                squares = part if squares is None else squares + part
            turned = block.T.reshape(width // GROUP, GROUP, span)
            turned = jnp.concatenate(
                [turned[:, :, part * lanes : (part + 1) * lanes] for part in range(parts)], axis=1
            )
            out_ref[tile * some : (tile + 1) * some, array] = turned.astype(jnp.bfloat16).reshape(
                some, groups, rows, lanes
            )
    sq_ref[...] = jnp.sum(squares.T, axis=0, keepdims=True)


def conv_kernel(in_ref, fo_ref, io_ref, fi_ref, ii_ref, cos_ref, sin_ref, out_ref):
    devices, _, groups, rows, lanes = in_ref.shape
    some = devices // RADIX
    size = some * rows
    few = size // GROUP

    def turn(re, im, j, sign):
        cos, sin = (
            jnp.broadcast_to(
                ref[j * few : (j + 1) * few][:, None, :], (few, GROUP, lanes)
            ).reshape(size, lanes)
            for ref in (cos_ref, sin_ref)
        )
        if sign > 0:
            return re * cos - im * sin, re * sin + im * cos
        return re * cos + im * sin, im * cos - re * sin

    def outer(group):
        blocks = []
        for q in range(RADIX):
            pair = [
                in_ref[q * some : (q + 1) * some, array, group].reshape(size, lanes)
                for array in range(2)
            ]
            blocks.append(jnp.concatenate(pair, axis=1).astype(jnp.float32))
        return [
            outer_dot(fo_ref[j], jnp.concatenate([re, im], axis=0))
            for j, (re, im) in enumerate(quarters(*blocks))
        ]

    def spectra(outers):
        turned = []
        for j, part in enumerate(outers):
            turned.append(
                [
                    jnp.concatenate(
                        turn(part[:size, at : at + lanes], part[size:, at : at + lanes], j, -1), axis=1
                    ).astype(jnp.bfloat16)
                    for at in (0, lanes)
                ]
            )
        return [dot(jnp.concatenate(part, axis=0), fi_ref[...]) for part in zip(*turned)]

    def product(sig, fil):
        sig_re, sig_im = sig[:, :lanes], sig[:, lanes:]
        fil_re, fil_im = fil[:, :lanes], fil[:, lanes:]
        prod = jnp.concatenate(
            [sig_re * fil_re - sig_im * fil_im, sig_re * fil_im + sig_im * fil_re], axis=1
        )
        return dot(prod.astype(jnp.bfloat16), ii_ref[...])

    def unturned(spread):
        results = []
        for j in range(RADIX):
            back = spread[j * size : (j + 1) * size]
            back = turn(back[:, :lanes], back[:, lanes:], j, 1)
            results.append(jnp.concatenate(back, axis=0).astype(jnp.bfloat16))
        return results

    def finish(group, first, second):
        parts = []
        for j, pair in enumerate(zip(first, second)):
            part = outer_dot(io_ref[j], jnp.concatenate(pair, axis=1))
            parts.append((part[:size], part[size:]))
        for q, conv in enumerate(recombined(parts)):
            conv = conv.astype(jnp.bfloat16)
            for half in range(2):
                out_ref[q * some : (q + 1) * some, group + half] = conv[
                    :, half * lanes : (half + 1) * lanes
                ].reshape(some, rows, lanes)

    outers = [outer(group) for group in range(groups)]
    specs = [spectra(part) for part in outers]
    spreads = [product(*spec) for spec in specs]
    results = [unturned(spread) for spread in spreads]
    for group in range(0, groups, 2):
        finish(group, results[group], results[group + 1])


def token_sums(terms):
    tokens, channels = terms.shape
    part = terms[:, :LANES]
    for start in range(LANES, channels, LANES):
        part = part + terms[:, start : start + LANES]
    return part


def finish_kernel(conv_ref, sig_ref, gate_ref, skip_ref, sq_ref, out_ref, sums_ref):
    devices, groups, rows, lanes = conv_ref.shape
    parts = rows // GROUP
    span, channels = out_ref.shape
    width, some = channels // TILES, devices // TILES
    sums = None
    for tile in range(TILES):
        turned = conv_ref[tile * some : (tile + 1) * some].astype(jnp.float32)
        turned = turned.reshape(some * groups, rows, lanes)
        conv = jnp.concatenate(
            [
                turned[:, part * GROUP : (part + 1) * GROUP].reshape(width, lanes).T
                for part in range(parts)
            ],
            axis=0,
        )
        at = slice(tile * width, (tile + 1) * width)
        sig = sig_ref[:, at].astype(jnp.float32)
        mixed = gate_ref[:, at].astype(jnp.float32) * (conv + skip_ref[:, at] * sig)
        out_ref[:, at] = mixed.astype(jnp.bfloat16)
        terms = [token_sums(sig * mixed), token_sums(mixed * mixed)]
        sums = terms if sums is None else [a + b for a, b in zip(sums, terms)]
    for row, total in enumerate(sums):
        sums_ref[row : row + 1] = jnp.sum(total.T, axis=0, keepdims=True)
    sums_ref[2:3] = sq_ref[...]


def deliver_kernel(in_ref, out_ref, sem_ref):
    copies = tile_copies(in_ref, out_ref, sem_ref)
    for copy in copies:
        copy.start()
    for copy in copies:
        copy.wait()


def call(kernel, out_shape, **kwargs):
    return pl.pallas_call(
        kernel,
        out_shape=out_shape,
        compiler_params=pltpu.CompilerParams(vmem_limit_bytes=VMEM_LIMIT),
        **kwargs,
    )


def local(signal, gating, filters, skip_gain):
    count = lax.axis_size("ctx")
    span, channels = signal.shape
    width = channels // count
    parts = span // LANES
    packed_tail = (width // GROUP, parts * GROUP, LANES)
    bf16, f32 = jnp.bfloat16, jnp.float32
    hbm = pl.BlockSpec(memory_space=pltpu.HBM)
    vmem = pl.BlockSpec(memory_space=pltpu.VMEM)
    tile_sems = pltpu.SemaphoreType.DMA((TILES,))
    packed, sig_sq = call(
        prepare_kernel,
        (
            jax.ShapeDtypeStruct((count, 2) + packed_tail, bf16),
            jax.ShapeDtypeStruct((1, span), f32),
        ),
        in_specs=[vmem, vmem],
        out_specs=(vmem, vmem),
    )(signal, filters.astype(bf16))
    chans, sections = lax.axis_size("chan"), lax.axis_size("section")
    last = sections - 1

    def total_first(part):
        total = part
        for hop in range(1, chans):
            total = total + lax.ppermute(
                part,
                ("chan", "section"),
                [(i * sections + last, (i + hop) % chans * sections + last) for i in range(chans)],
            )
        return total

    is_last = lax.axis_index("section") == last
    sig_sq = lax.cond(is_last, total_first, lambda part: part, sig_sq)
    packed, sig_sq = lax.optimization_barrier((packed, sig_sq))
    received = lax.all_to_all(packed, "ctx", split_axis=0, concat_axis=0, tiled=True)
    conv = call(conv_kernel, jax.ShapeDtypeStruct((count,) + packed_tail, bf16))(
        received, *conv_tables(count * parts, LANES)
    )
    returned = lax.all_to_all(conv, "ctx", split_axis=0, concat_axis=0, tiled=True)
    mixed, sums = call(
        finish_kernel,
        (jax.ShapeDtypeStruct((span, channels), bf16), jax.ShapeDtypeStruct((3, span), f32)),
        in_specs=[vmem] * 5,
        out_specs=(vmem, vmem),
    )(returned, signal, gating, skip_gain.reshape(1, channels), sig_sq)
    result = call(
        deliver_kernel,
        jax.ShapeDtypeStruct((span, channels), bf16),
        in_specs=[pl.BlockSpec(memory_space=pl.ANY)],
        out_specs=hbm,
        scratch_shapes=[tile_sems],
    )(mixed)
    reach = 2
    while reach <= chans:
        sums = sums + lax.ppermute(sums, "chan", [(i, i ^ (reach - 1)) for i in range(chans)])
        reach *= 2
    inner_total, out_total, sig_total = sums
    sig_total = jnp.where(is_last, sig_sq[0], sig_total)
    cosine = inner_total / jnp.sqrt((sig_total + EPSILON) * (out_total + EPSILON))
    return (result, cosine)


def solution(mesh):
    return jax.shard_map(
        local,
        mesh=mesh,
        in_specs=(
            P(("section", "ctx"), "chan"),
            P(("section", "ctx"), "chan"),
            P(("section", "ctx"), "chan"),
            P(("section", "chan")),
        ),
        out_specs=(P(("section", "ctx"), "chan"), P(("section", "ctx"))),
        check_vma=False,
    )
```

```python
import math

import jax
import jax.numpy as jnp
import ml_dtypes
import numpy as np
from jax import lax
from jax.experimental import pallas as pl
from jax.experimental.pallas import tpu as pltpu
from jax.sharding import PartitionSpec as P

EPSILON = 1e-06
VMEM_LIMIT = 20 * 2**20
LANES = 128
GROUP = 8
TILES = 4
RADIX = 4
COS, SIN, HALF = math.cos(math.pi / 8), math.sin(math.pi / 8), math.sqrt(0.5)


def two_parts(table):
    high = table.astype(ml_dtypes.bfloat16)
    low = (table - high.astype(np.float64)).astype(ml_dtypes.bfloat16)
    return np.concatenate([high, low], axis=-1)


def mild_scale(table):
    scales = 1 + np.arange(4000) / 4000
    errors = [
        np.square((scale * table).astype(ml_dtypes.bfloat16).astype(np.float64) / scale - table).mean()
        for scale in scales
    ]
    return scales[int(np.argmin(errors))]


def conv_tables(blocks, span):
    total = blocks * span
    few = blocks // RADIX
    m, r = np.arange(few), np.arange(span)
    k1 = RADIX * np.arange(few)[None, :] + np.arange(RADIX)[:, None]
    outer = 2 * np.pi * (4 * k1 + 1)[:, :, None] * m / (4 * blocks)
    twiddle = 2 * np.pi * (4 * k1 + 1).reshape(-1, 1) * r / (4 * total)
    inner = 2 * np.pi * np.outer(r, r) / span

    def split(cos, sin):
        return np.block([[cos, -sin], [sin, cos]])

    def spread(angles):
        eye = np.eye(GROUP)
        return split(np.kron(np.cos(angles), eye), np.kron(np.sin(angles), eye))

    inner_scale, outer_scale = mild_scale(np.cos(inner)), mild_scale(np.cos(outer))
    first_scale = (total * inner_scale**3 * outer_scale) ** -0.5
    fwd_outer = two_parts(first_scale * np.stack([spread(-angles) for angles in outer]))
    inv_outer = outer_scale * np.stack([spread(angles.T) for angles in outer])
    fwd_inner = inner_scale * split(np.cos(inner), np.sin(inner))
    inv_inner = inner_scale * split(np.cos(inner), -np.sin(inner))
    short = [fwd_outer] + [t.astype(ml_dtypes.bfloat16) for t in (inv_outer, fwd_inner, inv_inner)]
    wide = [np.cos(twiddle).astype(np.float32), np.sin(twiddle).astype(np.float32)]
    return short + wide


def quarters(x0, x1, x2, x3):
    even, odd = HALF * x2, (COS * x1, SIN * x1, COS * x3, SIN * x3)
    plus, minus = x0 + even, x0 - even
    c, d = odd[0] + odd[3], odd[1] - odd[2]
    e, f = odd[1] + odd[2], odd[0] - odd[3]
    return [
        (plus + c, -(e + even)),
        (minus - d, even - f),
        (plus - c, e - even),
        (minus + d, f + even),
    ]


def recombined(parts):
    (r0, i0), (r1, i1), (r2, i2), (r3, i3) = parts
    a, b, c, d = r0 - r2, r1 - r3, i0 - i2, i1 - i3
    e, f = r0 + r2, r1 + r3
    return [
        e + f,
        COS * (a - d) - SIN * (b + c),
        HALF * ((e - f) - ((i0 + i2) - (i1 + i3))),
        SIN * (a + d) + COS * (b - c),
    ]


def dot(left, right):
    return jnp.dot(left, right, preferred_element_type=jnp.float32)


def outer_dot(table, values):
    values = values.astype(jnp.bfloat16)
    return dot(table, jnp.concatenate([values, values], axis=0))


def tile_copies(hbm_ref, buf_ref, sem_ref):
    width = hbm_ref.shape[1] // TILES
    spans = [pl.ds(tile * width, width) for tile in range(TILES)]
    return [
        pltpu.make_async_copy(hbm_ref.at[:, span], buf_ref.at[:, span], sem_ref.at[tile])
        for tile, span in enumerate(spans)
    ]


def prepare_kernel(sig_ref, fil_ref, out_ref, sq_ref):
    devices, _, groups, rows, lanes = out_ref.shape
    parts = rows // GROUP
    span, channels = sig_ref.shape
    width, some = channels // TILES, devices // TILES
    squares = None
    for tile in range(TILES):
        for array, ref in enumerate((sig_ref, fil_ref)):
            block = ref[:, tile * width : (tile + 1) * width].astype(jnp.float32)
            if array == 0:
                part = token_sums(block * block)
                squares = part if squares is None else squares + part
            turned = block.T.reshape(width // GROUP, GROUP, span)
            turned = jnp.concatenate(
                [turned[:, :, part * lanes : (part + 1) * lanes] for part in range(parts)], axis=1
            )
            out_ref[tile * some : (tile + 1) * some, array] = turned.astype(jnp.bfloat16).reshape(
                some, groups, rows, lanes
            )
    sq_ref[...] = jnp.sum(squares.T, axis=0, keepdims=True)


def conv_kernel(in_ref, fo_ref, io_ref, fi_ref, ii_ref, cos_ref, sin_ref, out_ref):
    devices, _, groups, rows, lanes = in_ref.shape
    some = devices // RADIX
    size = some * rows
    few = size // GROUP

    def turn(re, im, j, sign):
        cos, sin = (
            jnp.broadcast_to(
                ref[j * few : (j + 1) * few][:, None, :], (few, GROUP, lanes)
            ).reshape(size, lanes)
            for ref in (cos_ref, sin_ref)
        )
        if sign > 0:
            return re * cos - im * sin, re * sin + im * cos
        return re * cos + im * sin, im * cos - re * sin

    def outer(group):
        blocks = []
        for q in range(RADIX):
            pair = [
                in_ref[q * some : (q + 1) * some, array, group].reshape(size, lanes)
                for array in range(2)
            ]
            blocks.append(jnp.concatenate(pair, axis=1).astype(jnp.float32))
        return [
            outer_dot(fo_ref[j], jnp.concatenate([re, im], axis=0))
            for j, (re, im) in enumerate(quarters(*blocks))
        ]

    def spectra(outers):
        turned = []
        for j, part in enumerate(outers):
            turned.append(
                [
                    jnp.concatenate(
                        turn(part[:size, at : at + lanes], part[size:, at : at + lanes], j, -1), axis=1
                    ).astype(jnp.bfloat16)
                    for at in (0, lanes)
                ]
            )
        return [dot(jnp.concatenate(part, axis=0), fi_ref[...]) for part in zip(*turned)]

    def product(sig, fil):
        sig_re, sig_im = sig[:, :lanes], sig[:, lanes:]
        fil_re, fil_im = fil[:, :lanes], fil[:, lanes:]
        prod = jnp.concatenate(
            [sig_re * fil_re - sig_im * fil_im, sig_re * fil_im + sig_im * fil_re], axis=1
        )
        return dot(prod.astype(jnp.bfloat16), ii_ref[...])

    def unturned(spread):
        results = []
        for j in range(RADIX):
            back = spread[j * size : (j + 1) * size]
            back = turn(back[:, :lanes], back[:, lanes:], j, 1)
            results.append(jnp.concatenate(back, axis=0).astype(jnp.bfloat16))
        return results

    def finish(group, first, second):
        parts = []
        for j, pair in enumerate(zip(first, second)):
            part = dot(io_ref[j], jnp.concatenate(pair, axis=1))
            parts.append((part[:size], part[size:]))
        for q, conv in enumerate(recombined(parts)):
            conv = conv.astype(jnp.bfloat16)
            for half in range(2):
                out_ref[q * some : (q + 1) * some, group + half] = conv[
                    :, half * lanes : (half + 1) * lanes
                ].reshape(some, rows, lanes)

    outers = [outer(group) for group in range(groups)]
    specs = [spectra(part) for part in outers]
    spreads = [product(*spec) for spec in specs]
    results = [unturned(spread) for spread in spreads]
    for group in range(0, groups, 2):
        finish(group, results[group], results[group + 1])


def token_sums(terms):
    tokens, channels = terms.shape
    part = terms[:, :LANES]
    for start in range(LANES, channels, LANES):
        part = part + terms[:, start : start + LANES]
    return part


def finish_kernel(conv_ref, sig_ref, gate_ref, skip_ref, sq_ref, out_ref, sums_ref):
    devices, groups, rows, lanes = conv_ref.shape
    parts = rows // GROUP
    span, channels = out_ref.shape
    width, some = channels // TILES, devices // TILES
    sums = None
    for tile in range(TILES):
        turned = conv_ref[tile * some : (tile + 1) * some].astype(jnp.float32)
        turned = turned.reshape(some * groups, rows, lanes)
        conv = jnp.concatenate(
            [
                turned[:, part * GROUP : (part + 1) * GROUP].reshape(width, lanes).T
                for part in range(parts)
            ],
            axis=0,
        )
        at = slice(tile * width, (tile + 1) * width)
        sig = sig_ref[:, at].astype(jnp.float32)
        mixed = gate_ref[:, at].astype(jnp.float32) * (conv + skip_ref[:, at] * sig)
        out_ref[:, at] = mixed.astype(jnp.bfloat16)
        terms = [token_sums(sig * mixed), token_sums(mixed * mixed)]
        sums = terms if sums is None else [a + b for a, b in zip(sums, terms)]
    for row, total in enumerate(sums):
        sums_ref[row : row + 1] = jnp.sum(total.T, axis=0, keepdims=True)
    sums_ref[2:3] = sq_ref[...]


def deliver_kernel(in_ref, out_ref, sem_ref):
    copies = tile_copies(in_ref, out_ref, sem_ref)
    for copy in copies:
        copy.start()
    for copy in copies:
        copy.wait()


def call(kernel, out_shape, **kwargs):
    return pl.pallas_call(
        kernel,
        out_shape=out_shape,
        compiler_params=pltpu.CompilerParams(vmem_limit_bytes=VMEM_LIMIT),
        **kwargs,
    )


def local(signal, gating, filters, skip_gain):
    count = lax.axis_size("ctx")
    span, channels = signal.shape
    width = channels // count
    parts = span // LANES
    packed_tail = (width // GROUP, parts * GROUP, LANES)
    bf16, f32 = jnp.bfloat16, jnp.float32
    hbm = pl.BlockSpec(memory_space=pltpu.HBM)
    vmem = pl.BlockSpec(memory_space=pltpu.VMEM)
    tile_sems = pltpu.SemaphoreType.DMA((TILES,))
    packed, sig_sq = call(
        prepare_kernel,
        (
            jax.ShapeDtypeStruct((count, 2) + packed_tail, bf16),
            jax.ShapeDtypeStruct((1, span), f32),
        ),
        in_specs=[vmem, vmem],
        out_specs=(vmem, vmem),
    )(signal, filters.astype(bf16))
    chans, sections = lax.axis_size("chan"), lax.axis_size("section")
    last = sections - 1

    def total_first(part):
        total = part
        for hop in range(1, chans):
            total = total + lax.ppermute(
                part,
                ("chan", "section"),
                [(i * sections + last, (i + hop) % chans * sections + last) for i in range(chans)],
            )
        return total

    is_last = lax.axis_index("section") == last
    sig_sq = lax.cond(is_last, total_first, lambda part: part, sig_sq)
    packed, sig_sq = lax.optimization_barrier((packed, sig_sq))
    received = lax.all_to_all(packed, "ctx", split_axis=0, concat_axis=0, tiled=True)
    conv = call(conv_kernel, jax.ShapeDtypeStruct((count,) + packed_tail, bf16))(
        received, *conv_tables(count * parts, LANES)
    )
    returned = lax.all_to_all(conv, "ctx", split_axis=0, concat_axis=0, tiled=True)
    mixed, sums = call(
        finish_kernel,
        (jax.ShapeDtypeStruct((span, channels), bf16), jax.ShapeDtypeStruct((3, span), f32)),
        in_specs=[vmem] * 5,
        out_specs=(vmem, vmem),
    )(returned, signal, gating, skip_gain.reshape(1, channels), sig_sq)
    result = call(
        deliver_kernel,
        jax.ShapeDtypeStruct((span, channels), bf16),
        in_specs=[pl.BlockSpec(memory_space=pl.ANY)],
        out_specs=hbm,
        scratch_shapes=[tile_sems],
    )(mixed)
    reach = 2
    while reach <= chans:
        sums = sums + lax.ppermute(sums, "chan", [(i, i ^ (reach - 1)) for i in range(chans)])
        reach *= 2
    inner_total, out_total, sig_total = sums
    sig_total = jnp.where(is_last, sig_sq[0], sig_total)
    cosine = inner_total / jnp.sqrt((sig_total + EPSILON) * (out_total + EPSILON))
    return (result, cosine)


def solution(mesh):
    return jax.shard_map(
        local,
        mesh=mesh,
        in_specs=(
            P(("section", "ctx"), "chan"),
            P(("section", "ctx"), "chan"),
            P(("section", "ctx"), "chan"),
            P(("section", "chan")),
        ),
        out_specs=(P(("section", "ctx"), "chan"), P(("section", "ctx"))),
        check_vma=False,
    )
```

```python
import math

import jax
import jax.numpy as jnp
import ml_dtypes
import numpy as np
from jax import lax
from jax.experimental import pallas as pl
from jax.experimental.pallas import tpu as pltpu
from jax.sharding import PartitionSpec as P

EPSILON = 1e-06
VMEM_LIMIT = 20 * 2**20
LANES = 128
GROUP = 8
TILES = 4
RADIX = 4
COS, SIN, HALF = math.cos(math.pi / 8), math.sin(math.pi / 8), math.sqrt(0.5)


def two_parts(table):
    high = table.astype(ml_dtypes.bfloat16)
    low = (table - high.astype(np.float64)).astype(ml_dtypes.bfloat16)
    return np.concatenate([high, low], axis=-2)


def mild_scale(table):
    scales = 1 + np.arange(4000) / 4000
    errors = [
        np.square((scale * table).astype(ml_dtypes.bfloat16).astype(np.float64) / scale - table).mean()
        for scale in scales
    ]
    return scales[int(np.argmin(errors))]


def conv_tables(blocks, span):
    total = blocks * span
    few = blocks // RADIX
    m, r = np.arange(few), np.arange(span)
    k1 = RADIX * np.arange(few)[None, :] + np.arange(RADIX)[:, None]
    outer = 2 * np.pi * (4 * k1 + 1)[:, :, None] * m / (4 * blocks)
    twiddle = 2 * np.pi * (4 * k1 + 1).reshape(-1, 1) * r / (4 * total)
    inner = 2 * np.pi * np.outer(r, r) / span

    def split(cos, sin):
        return np.block([[cos, -sin], [sin, cos]])

    def spread(angles):
        eye = np.eye(GROUP)
        return split(np.kron(np.cos(angles), eye), np.kron(np.sin(angles), eye))

    inner_scale, outer_scale = mild_scale(np.cos(inner)), mild_scale(np.cos(outer))
    first_scale = (total * inner_scale**3 * outer_scale) ** -0.5
    fwd_outer = two_parts(first_scale * np.stack([spread(-angles) for angles in outer]))
    inv_outer = outer_scale * np.stack([spread(angles.T) for angles in outer])
    fwd_inner = inner_scale * split(np.cos(inner), np.sin(inner))
    inv_inner = inner_scale * split(np.cos(inner), -np.sin(inner))
    short = [fwd_outer] + [t.astype(ml_dtypes.bfloat16) for t in (inv_outer, fwd_inner, inv_inner)]
    wide = [np.cos(twiddle).astype(np.float32), np.sin(twiddle).astype(np.float32)]
    return short + wide


def quarters(x0, x1, x2, x3):
    even, odd = HALF * x2, (COS * x1, SIN * x1, COS * x3, SIN * x3)
    plus, minus = x0 + even, x0 - even
    c, d = odd[0] + odd[3], odd[1] - odd[2]
    e, f = odd[1] + odd[2], odd[0] - odd[3]
    return [
        (plus + c, -(e + even)),
        (minus - d, even - f),
        (plus - c, e - even),
        (minus + d, f + even),
    ]


def recombined(parts):
    (r0, i0), (r1, i1), (r2, i2), (r3, i3) = parts
    a, b, c, d = r0 - r2, r1 - r3, i0 - i2, i1 - i3
    e, f = r0 + r2, r1 + r3
    return [
        e + f,
        COS * (a - d) - SIN * (b + c),
        HALF * ((e - f) - ((i0 + i2) - (i1 + i3))),
        SIN * (a + d) + COS * (b - c),
    ]


def dot(left, right):
    return jnp.dot(left, right, preferred_element_type=jnp.float32)


def outer_dot(table, values):
    both = dot(table, values.astype(jnp.bfloat16))
    half = both.shape[0] // 2
    return both[:half] + both[half:]


def tile_copies(hbm_ref, buf_ref, sem_ref):
    width = hbm_ref.shape[1] // TILES
    spans = [pl.ds(tile * width, width) for tile in range(TILES)]
    return [
        pltpu.make_async_copy(hbm_ref.at[:, span], buf_ref.at[:, span], sem_ref.at[tile])
        for tile, span in enumerate(spans)
    ]


def prepare_kernel(sig_ref, fil_ref, out_ref, sq_ref):
    devices, _, groups, rows, lanes = out_ref.shape
    parts = rows // GROUP
    span, channels = sig_ref.shape
    width, some = channels // TILES, devices // TILES
    squares = None
    for tile in range(TILES):
        for array, ref in enumerate((sig_ref, fil_ref)):
            block = ref[:, tile * width : (tile + 1) * width].astype(jnp.float32)
            if array == 0:
                part = token_sums(block * block)
                squares = part if squares is None else squares + part
            turned = block.T.reshape(width // GROUP, GROUP, span)
            turned = jnp.concatenate(
                [turned[:, :, part * lanes : (part + 1) * lanes] for part in range(parts)], axis=1
            )
            out_ref[tile * some : (tile + 1) * some, array] = turned.astype(jnp.bfloat16).reshape(
                some, groups, rows, lanes
            )
    sq_ref[...] = jnp.sum(squares.T, axis=0, keepdims=True)


def conv_kernel(in_ref, fo_ref, io_ref, fi_ref, ii_ref, cos_ref, sin_ref, out_ref):
    devices, _, groups, rows, lanes = in_ref.shape
    some = devices // RADIX
    size = some * rows
    few = size // GROUP

    def turn(re, im, j, sign):
        cos, sin = (
            jnp.broadcast_to(
                ref[j * few : (j + 1) * few][:, None, :], (few, GROUP, lanes)
            ).reshape(size, lanes)
            for ref in (cos_ref, sin_ref)
        )
        if sign > 0:
            return re * cos - im * sin, re * sin + im * cos
        return re * cos + im * sin, im * cos - re * sin

    def outer(group):
        blocks = []
        for q in range(RADIX):
            pair = [
                in_ref[q * some : (q + 1) * some, array, group].reshape(size, lanes)
                for array in range(2)
            ]
            blocks.append(jnp.concatenate(pair, axis=1).astype(jnp.float32))
        return [
            outer_dot(fo_ref[j], jnp.concatenate([re, im], axis=0))
            for j, (re, im) in enumerate(quarters(*blocks))
        ]

    def spectra(outers):
        turned = []
        for j, part in enumerate(outers):
            turned.append(
                [
                    jnp.concatenate(
                        turn(part[:size, at : at + lanes], part[size:, at : at + lanes], j, -1), axis=1
                    ).astype(jnp.bfloat16)
                    for at in (0, lanes)
                ]
            )
        return [dot(jnp.concatenate(part, axis=0), fi_ref[...]) for part in zip(*turned)]

    def product(sig, fil):
        sig_re, sig_im = sig[:, :lanes], sig[:, lanes:]
        fil_re, fil_im = fil[:, :lanes], fil[:, lanes:]
        prod = jnp.concatenate(
            [sig_re * fil_re - sig_im * fil_im, sig_re * fil_im + sig_im * fil_re], axis=1
        )
        return dot(prod.astype(jnp.bfloat16), ii_ref[...])

    def unturned(spread):
        results = []
        for j in range(RADIX):
            back = spread[j * size : (j + 1) * size]
            back = turn(back[:, :lanes], back[:, lanes:], j, 1)
            results.append(jnp.concatenate(back, axis=0).astype(jnp.bfloat16))
        return results

    def finish(group, first, second):
        parts = []
        for j, pair in enumerate(zip(first, second)):
            part = dot(io_ref[j], jnp.concatenate(pair, axis=1))
            parts.append((part[:size], part[size:]))
        for q, conv in enumerate(recombined(parts)):
            conv = conv.astype(jnp.bfloat16)
            for half in range(2):
                out_ref[q * some : (q + 1) * some, group + half] = conv[
                    :, half * lanes : (half + 1) * lanes
                ].reshape(some, rows, lanes)

    outers = [outer(group) for group in range(groups)]
    specs = [spectra(part) for part in outers]
    spreads = [product(*spec) for spec in specs]
    results = [unturned(spread) for spread in spreads]
    for group in range(0, groups, 2):
        finish(group, results[group], results[group + 1])


def token_sums(terms):
    tokens, channels = terms.shape
    part = terms[:, :LANES]
    for start in range(LANES, channels, LANES):
        part = part + terms[:, start : start + LANES]
    return part


def finish_kernel(conv_ref, sig_ref, gate_ref, skip_ref, sq_ref, out_ref, sums_ref):
    devices, groups, rows, lanes = conv_ref.shape
    parts = rows // GROUP
    span, channels = out_ref.shape
    width, some = channels // TILES, devices // TILES
    sums = None
    for tile in range(TILES):
        turned = conv_ref[tile * some : (tile + 1) * some].astype(jnp.float32)
        turned = turned.reshape(some * groups, rows, lanes)
        conv = jnp.concatenate(
            [
                turned[:, part * GROUP : (part + 1) * GROUP].reshape(width, lanes).T
                for part in range(parts)
            ],
            axis=0,
        )
        at = slice(tile * width, (tile + 1) * width)
        sig = sig_ref[:, at].astype(jnp.float32)
        mixed = gate_ref[:, at].astype(jnp.float32) * (conv + skip_ref[:, at] * sig)
        out_ref[:, at] = mixed.astype(jnp.bfloat16)
        terms = [token_sums(sig * mixed), token_sums(mixed * mixed)]
        sums = terms if sums is None else [a + b for a, b in zip(sums, terms)]
    for row, total in enumerate(sums):
        sums_ref[row : row + 1] = jnp.sum(total.T, axis=0, keepdims=True)
    sums_ref[2:3] = sq_ref[...]


def deliver_kernel(in_ref, out_ref, sem_ref):
    copies = tile_copies(in_ref, out_ref, sem_ref)
    for copy in copies:
        copy.start()
    for copy in copies:
        copy.wait()


def call(kernel, out_shape, **kwargs):
    return pl.pallas_call(
        kernel,
        out_shape=out_shape,
        compiler_params=pltpu.CompilerParams(vmem_limit_bytes=VMEM_LIMIT),
        **kwargs,
    )


def local(signal, gating, filters, skip_gain):
    count = lax.axis_size("ctx")
    span, channels = signal.shape
    width = channels // count
    parts = span // LANES
    packed_tail = (width // GROUP, parts * GROUP, LANES)
    bf16, f32 = jnp.bfloat16, jnp.float32
    hbm = pl.BlockSpec(memory_space=pltpu.HBM)
    vmem = pl.BlockSpec(memory_space=pltpu.VMEM)
    tile_sems = pltpu.SemaphoreType.DMA((TILES,))
    packed, sig_sq = call(
        prepare_kernel,
        (
            jax.ShapeDtypeStruct((count, 2) + packed_tail, bf16),
            jax.ShapeDtypeStruct((1, span), f32),
        ),
        in_specs=[vmem, vmem],
        out_specs=(vmem, vmem),
    )(signal, filters.astype(bf16))
    chans, sections = lax.axis_size("chan"), lax.axis_size("section")
    last = sections - 1

    def total_first(part):
        total = part
        for hop in range(1, chans):
            total = total + lax.ppermute(
                part,
                ("chan", "section"),
                [(i * sections + last, (i + hop) % chans * sections + last) for i in range(chans)],
            )
        return total

    is_last = lax.axis_index("section") == last
    sig_sq = lax.cond(is_last, total_first, lambda part: part, sig_sq)
    packed, sig_sq = lax.optimization_barrier((packed, sig_sq))
    received = lax.all_to_all(packed, "ctx", split_axis=0, concat_axis=0, tiled=True)
    conv = call(conv_kernel, jax.ShapeDtypeStruct((count,) + packed_tail, bf16))(
        received, *conv_tables(count * parts, LANES)
    )
    returned = lax.all_to_all(conv, "ctx", split_axis=0, concat_axis=0, tiled=True)
    mixed, sums = call(
        finish_kernel,
        (jax.ShapeDtypeStruct((span, channels), bf16), jax.ShapeDtypeStruct((3, span), f32)),
        in_specs=[vmem] * 5,
        out_specs=(vmem, vmem),
    )(returned, signal, gating, skip_gain.reshape(1, channels), sig_sq)
    result = call(
        deliver_kernel,
        jax.ShapeDtypeStruct((span, channels), bf16),
        in_specs=[pl.BlockSpec(memory_space=pl.ANY)],
        out_specs=hbm,
        scratch_shapes=[tile_sems],
    )(mixed)
    reach = 2
    while reach <= chans:
        sums = sums + lax.ppermute(sums, "chan", [(i, i ^ (reach - 1)) for i in range(chans)])
        reach *= 2
    inner_total, out_total, sig_total = sums
    sig_total = jnp.where(is_last, sig_sq[0], sig_total)
    cosine = inner_total / jnp.sqrt((sig_total + EPSILON) * (out_total + EPSILON))
    return (result, cosine)


def solution(mesh):
    return jax.shard_map(
        local,
        mesh=mesh,
        in_specs=(
            P(("section", "ctx"), "chan"),
            P(("section", "ctx"), "chan"),
            P(("section", "ctx"), "chan"),
            P(("section", "chan")),
        ),
        out_specs=(P(("section", "ctx"), "chan"), P(("section", "ctx"))),
        check_vma=False,
    )
```

```python
import math

import jax
import jax.numpy as jnp
import ml_dtypes
import numpy as np
from jax import lax
from jax.experimental import pallas as pl
from jax.experimental.pallas import tpu as pltpu
from jax.sharding import PartitionSpec as P

EPSILON = 1e-06
VMEM_LIMIT = 20 * 2**20
LANES = 128
GROUP = 8
TILES = 4
RADIX = 4
COS, SIN, HALF = math.cos(math.pi / 8), math.sin(math.pi / 8), math.sqrt(0.5)


def two_parts(table):
    high = table.astype(ml_dtypes.bfloat16)
    low = (table - high.astype(np.float64)).astype(ml_dtypes.bfloat16)
    return np.concatenate([high, low], axis=-2)


def mild_scale(table):
    scales = 1 + np.arange(4000) / 4000
    errors = [
        np.square((scale * table).astype(ml_dtypes.bfloat16).astype(np.float64) / scale - table).mean()
        for scale in scales
    ]
    return scales[int(np.argmin(errors))]


def conv_tables(blocks, span):
    total = blocks * span
    few = blocks // RADIX
    m, r = np.arange(few), np.arange(span)
    k1 = RADIX * np.arange(few)[None, :] + np.arange(RADIX)[:, None]
    outer = 2 * np.pi * (4 * k1 + 1)[:, :, None] * m / (4 * blocks)
    twiddle = 2 * np.pi * (4 * k1 + 1).reshape(-1, 1) * r / (4 * total)
    inner = 2 * np.pi * np.outer(r, r) / span

    def split(cos, sin):
        return np.block([[cos, -sin], [sin, cos]])

    def spread(angles):
        eye = np.eye(GROUP)
        return split(np.kron(np.cos(angles), eye), np.kron(np.sin(angles), eye))

    inner_scale, outer_scale = mild_scale(np.cos(inner)), mild_scale(np.cos(outer))
    first_scale = (total * inner_scale**3 * outer_scale) ** -0.5
    fwd_outer = two_parts(first_scale * np.stack([spread(-angles) for angles in outer]))
    inv_outer = outer_scale * np.stack([spread(angles.T) for angles in outer])
    fwd_inner = inner_scale * split(np.cos(inner), np.sin(inner))
    inv_inner = inner_scale * split(np.cos(inner), -np.sin(inner))
    short = [fwd_outer] + [t.astype(ml_dtypes.bfloat16) for t in (inv_outer, fwd_inner, inv_inner)]
    wide = [np.cos(twiddle).astype(np.float32), np.sin(twiddle).astype(np.float32)]
    return short + wide


def quarters(x0, x1, x2, x3):
    even, odd = HALF * x2, (COS * x1, SIN * x1, COS * x3, SIN * x3)
    plus, minus = x0 + even, x0 - even
    c, d = odd[0] + odd[3], odd[1] - odd[2]
    e, f = odd[1] + odd[2], odd[0] - odd[3]
    return [
        (plus + c, -(e + even)),
        (minus - d, even - f),
        (plus - c, e - even),
        (minus + d, f + even),
    ]


def recombined(parts):
    (r0, i0), (r1, i1), (r2, i2), (r3, i3) = parts
    a, b, c, d = r0 - r2, r1 - r3, i0 - i2, i1 - i3
    e, f = r0 + r2, r1 + r3
    return [
        e + f,
        COS * (a - d) - SIN * (b + c),
        HALF * ((e - f) - ((i0 + i2) - (i1 + i3))),
        SIN * (a + d) + COS * (b - c),
    ]


def dot(left, right):
    return jnp.dot(left, right, preferred_element_type=jnp.float32)


def outer_dot(table, values):
    both = dot(table, values.astype(jnp.bfloat16))
    half = both.shape[0] // 2
    return both[:half] + both[half:]


def tile_copies(hbm_ref, buf_ref, sem_ref):
    width = hbm_ref.shape[1] // TILES
    spans = [pl.ds(tile * width, width) for tile in range(TILES)]
    return [
        pltpu.make_async_copy(hbm_ref.at[:, span], buf_ref.at[:, span], sem_ref.at[tile])
        for tile, span in enumerate(spans)
    ]


def prepare_kernel(sig_ref, fil_ref, out_ref, sq_ref):
    devices, _, groups, rows, lanes = out_ref.shape
    parts = rows // GROUP
    span, channels = sig_ref.shape
    width, some = channels // TILES, devices // TILES
    squares = None
    for tile in range(TILES):
        for array, ref in enumerate((sig_ref, fil_ref)):
            block = ref[:, tile * width : (tile + 1) * width].astype(jnp.float32)
            if array == 0:
                part = token_sums(block * block)
                squares = part if squares is None else squares + part
            turned = block.T.reshape(width // GROUP, GROUP, span)
            turned = jnp.concatenate(
                [turned[:, :, part * lanes : (part + 1) * lanes] for part in range(parts)], axis=1
            )
            out_ref[tile * some : (tile + 1) * some, array] = turned.astype(jnp.bfloat16).reshape(
                some, groups, rows, lanes
            )
    sq_ref[...] = jnp.sum(squares.T, axis=0, keepdims=True)


def conv_kernel(in_ref, fo_ref, io_ref, fi_ref, ii_ref, cos_ref, sin_ref, out_ref):
    devices, _, groups, rows, lanes = in_ref.shape
    some = devices // RADIX
    size = some * rows
    few = size // GROUP

    def turn(re, im, j, sign):
        cos, sin = (
            jnp.broadcast_to(
                ref[j * few : (j + 1) * few][:, None, :], (few, GROUP, lanes)
            ).reshape(size, lanes)
            for ref in (cos_ref, sin_ref)
        )
        if sign > 0:
            return re * cos - im * sin, re * sin + im * cos
        return re * cos + im * sin, im * cos - re * sin

    def outer(group):
        blocks = []
        for q in range(RADIX):
            pair = [
                in_ref[q * some : (q + 1) * some, array, group].reshape(size, lanes)
                for array in range(2)
            ]
            blocks.append(jnp.concatenate(pair, axis=1).astype(jnp.float32))
        return [
            outer_dot(fo_ref[j], jnp.concatenate([re, im], axis=0))
            for j, (re, im) in enumerate(quarters(*blocks))
        ]

    def spectra(outers):
        turned = []
        for j, part in enumerate(outers):
            turned.append(
                [
                    jnp.concatenate(
                        turn(part[:size, at : at + lanes], part[size:, at : at + lanes], j, -1), axis=1
                    ).astype(jnp.bfloat16)
                    for at in (0, lanes)
                ]
            )
        return [dot(jnp.concatenate(part, axis=0), fi_ref[...]) for part in zip(*turned)]

    def product(sig, fil):
        sig_re, sig_im = sig[:, :lanes], sig[:, lanes:]
        fil_re, fil_im = fil[:, :lanes], fil[:, lanes:]
        prod = jnp.concatenate(
            [sig_re * fil_re - sig_im * fil_im, sig_re * fil_im + sig_im * fil_re], axis=1
        )
        return dot(prod.astype(jnp.bfloat16), ii_ref[...])

    def unturned(spread):
        results = []
        for j in range(RADIX):
            back = spread[j * size : (j + 1) * size]
            back = turn(back[:, :lanes], back[:, lanes:], j, 1)
            results.append(jnp.concatenate(back, axis=0).astype(jnp.bfloat16))
        return results

    def finish(group, first, second):
        parts = []
        for j, pair in enumerate(zip(first, second)):
            part = dot(io_ref[j], jnp.concatenate(pair, axis=1))
            parts.append((part[:size], part[size:]))
        for q, conv in enumerate(recombined(parts)):
            conv = conv.astype(jnp.bfloat16)
            for half in range(2):
                out_ref[q * some : (q + 1) * some, group + half] = conv[
                    :, half * lanes : (half + 1) * lanes
                ].reshape(some, rows, lanes)

    outers = [outer(group) for group in range(groups)]
    specs = [spectra(part) for part in outers]
    spreads = [product(*spec) for spec in specs]
    results = [unturned(spread) for spread in spreads]
    for group in range(0, groups, 2):
        finish(group, results[group], results[group + 1])


def token_sums(terms):
    tokens, channels = terms.shape
    part = terms[:, :LANES]
    for start in range(LANES, channels, LANES):
        part = part + terms[:, start : start + LANES]
    return part


def finish_kernel(conv_ref, sig_ref, gate_ref, skip_ref, sq_ref, out_ref, sums_ref):
    devices, groups, rows, lanes = conv_ref.shape
    parts = rows // GROUP
    span, channels = out_ref.shape
    width, some = channels // TILES, devices // TILES
    sums = None
    for tile in range(TILES):
        turned = conv_ref[tile * some : (tile + 1) * some].astype(jnp.float32)
        turned = turned.reshape(some * groups, rows, lanes)
        conv = jnp.concatenate(
            [
                turned[:, part * GROUP : (part + 1) * GROUP].reshape(width, lanes).T
                for part in range(parts)
            ],
            axis=0,
        )
        at = slice(tile * width, (tile + 1) * width)
        sig = sig_ref[:, at].astype(jnp.float32)
        mixed = gate_ref[:, at].astype(jnp.float32) * (conv + skip_ref[:, at] * sig)
        out_ref[:, at] = mixed.astype(jnp.bfloat16)
        terms = [token_sums(sig * mixed), token_sums(mixed * mixed)]
        sums = terms if sums is None else [a + b for a, b in zip(sums, terms)]
    for row, total in enumerate(sums):
        sums_ref[row : row + 1] = jnp.sum(total.T, axis=0, keepdims=True)
    sums_ref[2:3] = sq_ref[...]


def deliver_kernel(in_ref, out_ref, sem_ref):
    copies = tile_copies(in_ref, out_ref, sem_ref)
    for copy in copies:
        copy.start()
    for copy in copies:
        copy.wait()


def call(kernel, out_shape, **kwargs):
    return pl.pallas_call(
        kernel,
        out_shape=out_shape,
        compiler_params=pltpu.CompilerParams(vmem_limit_bytes=VMEM_LIMIT),
        **kwargs,
    )


def local(signal, gating, filters, skip_gain):
    count = lax.axis_size("ctx")
    span, channels = signal.shape
    width = channels // count
    parts = span // LANES
    packed_tail = (width // GROUP, parts * GROUP, LANES)
    bf16, f32 = jnp.bfloat16, jnp.float32
    hbm = pl.BlockSpec(memory_space=pltpu.HBM)
    vmem = pl.BlockSpec(memory_space=pltpu.VMEM)
    tile_sems = pltpu.SemaphoreType.DMA((TILES,))
    packed, sig_sq = call(
        prepare_kernel,
        (
            jax.ShapeDtypeStruct((count, 2) + packed_tail, bf16),
            jax.ShapeDtypeStruct((1, span), f32),
        ),
        in_specs=[vmem, vmem],
        out_specs=(vmem, vmem),
    )(signal, filters.astype(bf16))
    chans, sections = lax.axis_size("chan"), lax.axis_size("section")
    last = sections - 1

    def total_first(part):
        total = part
        for hop in range(1, chans):
            total = total + lax.ppermute(
                part,
                ("chan", "section"),
                [(i * sections + last, (i + hop) % chans * sections + last) for i in range(chans)],
            )
        return total

    is_last = lax.axis_index("section") == last
    sig_sq = lax.cond(is_last, total_first, lambda part: part, sig_sq)
    packed, sig_sq = lax.optimization_barrier((packed, sig_sq))
    received = lax.all_to_all(packed, "ctx", split_axis=0, concat_axis=0, tiled=True)
    conv = call(conv_kernel, jax.ShapeDtypeStruct((count,) + packed_tail, bf16))(
        received, *conv_tables(count * parts, LANES)
    )
    returned = lax.all_to_all(conv, "ctx", split_axis=0, concat_axis=0, tiled=True)
    mixed, sums = call(
        finish_kernel,
        (jax.ShapeDtypeStruct((span, channels), bf16), jax.ShapeDtypeStruct((3, span), f32)),
        in_specs=[vmem] * 5,
        out_specs=(vmem, vmem),
    )(returned, signal, gating, skip_gain.reshape(1, channels), sig_sq)
    result = call(
        deliver_kernel,
        jax.ShapeDtypeStruct((span, channels), bf16),
        in_specs=[pl.BlockSpec(memory_space=pl.ANY)],
        out_specs=hbm,
        scratch_shapes=[tile_sems],
    )(mixed)
    reach = chans
    while reach > 1:
        sums = sums + lax.ppermute(sums, "chan", [(i, i ^ (reach - 1)) for i in range(chans)])
        reach //= 2
    inner_total, out_total, sig_total = sums
    sig_total = jnp.where(is_last, sig_sq[0], sig_total)
    cosine = inner_total / jnp.sqrt((sig_total + EPSILON) * (out_total + EPSILON))
    return (result, cosine)


def solution(mesh):
    return jax.shard_map(
        local,
        mesh=mesh,
        in_specs=(
            P(("section", "ctx"), "chan"),
            P(("section", "ctx"), "chan"),
            P(("section", "ctx"), "chan"),
            P(("section", "chan")),
        ),
        out_specs=(P(("section", "ctx"), "chan"), P(("section", "ctx"))),
        check_vma=False,
    )
```

```python
import math

import jax
import jax.numpy as jnp
import ml_dtypes
import numpy as np
from jax import lax
from jax.experimental import pallas as pl
from jax.experimental.pallas import tpu as pltpu
from jax.sharding import PartitionSpec as P

EPSILON = 1e-06
VMEM_LIMIT = 20 * 2**20
LANES = 128
GROUP = 8
TILES = 4
RADIX = 4
COS, SIN, HALF = math.cos(math.pi / 8), math.sin(math.pi / 8), math.sqrt(0.5)


def two_parts(table):
    high = table.astype(ml_dtypes.bfloat16)
    low = (table - high.astype(np.float64)).astype(ml_dtypes.bfloat16)
    return np.concatenate([high, low], axis=-2)


def mild_scale(table):
    scales = 1 + np.arange(4000) / 4000
    errors = [
        np.square((scale * table).astype(ml_dtypes.bfloat16).astype(np.float64) / scale - table).mean()
        for scale in scales
    ]
    return scales[int(np.argmin(errors))]


def conv_tables(blocks, span):
    total = blocks * span
    few = blocks // RADIX
    m, r = np.arange(few), np.arange(span)
    k1 = RADIX * np.arange(few)[None, :] + np.arange(RADIX)[:, None]
    outer = 2 * np.pi * (4 * k1 + 1)[:, :, None] * m / (4 * blocks)
    twiddle = 2 * np.pi * (4 * k1 + 1).reshape(-1, 1) * r / (4 * total)
    inner = 2 * np.pi * np.outer(r, r) / span

    def split(cos, sin):
        return np.block([[cos, -sin], [sin, cos]])

    def spread(angles):
        eye = np.eye(GROUP)
        return split(np.kron(np.cos(angles), eye), np.kron(np.sin(angles), eye))

    inner_scale, outer_scale = mild_scale(np.cos(inner)), mild_scale(np.cos(outer))
    first_scale = (total * inner_scale**3 * outer_scale) ** -0.5
    fwd_outer = two_parts(first_scale * np.stack([spread(-angles) for angles in outer]))
    inv_outer = outer_scale * np.stack([spread(angles.T) for angles in outer])
    fwd_inner = inner_scale * split(np.cos(inner), np.sin(inner))
    inv_inner = inner_scale * split(np.cos(inner), -np.sin(inner))
    short = [fwd_outer] + [t.astype(ml_dtypes.bfloat16) for t in (inv_outer, fwd_inner, inv_inner)]
    wide = [np.cos(twiddle).astype(np.float32), np.sin(twiddle).astype(np.float32)]
    return short + wide


def quarters(x0, x1, x2, x3):
    even, odd = HALF * x2, (COS * x1, SIN * x1, COS * x3, SIN * x3)
    plus, minus = x0 + even, x0 - even
    c, d = odd[0] + odd[3], odd[1] - odd[2]
    e, f = odd[1] + odd[2], odd[0] - odd[3]
    return [
        (plus + c, -(e + even)),
        (minus - d, even - f),
        (plus - c, e - even),
        (minus + d, f + even),
    ]


def recombined(parts):
    (r0, i0), (r1, i1), (r2, i2), (r3, i3) = parts
    a, b, c, d = r0 - r2, r1 - r3, i0 - i2, i1 - i3
    e, f = r0 + r2, r1 + r3
    return [
        e + f,
        COS * (a - d) - SIN * (b + c),
        HALF * ((e - f) - ((i0 + i2) - (i1 + i3))),
        SIN * (a + d) + COS * (b - c),
    ]


def dot(left, right):
    return jnp.dot(left, right, preferred_element_type=jnp.float32)


def outer_dot(table, values):
    both = dot(table, values.astype(jnp.bfloat16))
    half = both.shape[0] // 2
    return both[:half] + both[half:]


def tile_copies(hbm_ref, buf_ref, sem_ref):
    width = hbm_ref.shape[1] // TILES
    spans = [pl.ds(tile * width, width) for tile in range(TILES)]
    return [
        pltpu.make_async_copy(hbm_ref.at[:, span], buf_ref.at[:, span], sem_ref.at[tile])
        for tile, span in enumerate(spans)
    ]


def prepare_kernel(sig_ref, fil_ref, out_ref, sq_ref):
    devices, _, groups, rows, lanes = out_ref.shape
    parts = rows // GROUP
    span, channels = sig_ref.shape
    width, some = channels // TILES, devices // TILES
    squares = None
    for tile in range(TILES):
        for array, ref in enumerate((sig_ref, fil_ref)):
            block = ref[:, tile * width : (tile + 1) * width].astype(jnp.float32)
            if array == 0:
                part = token_sums(block * block)
                squares = part if squares is None else squares + part
            turned = block.T.reshape(width // GROUP, GROUP, span)
            turned = jnp.concatenate(
                [turned[:, :, part * lanes : (part + 1) * lanes] for part in range(parts)], axis=1
            )
            out_ref[tile * some : (tile + 1) * some, array] = turned.astype(jnp.bfloat16).reshape(
                some, groups, rows, lanes
            )
    sq_ref[...] = jnp.sum(squares.T, axis=0, keepdims=True)


def conv_kernel(in_ref, fo_ref, io_ref, fi_ref, ii_ref, cos_ref, sin_ref, out_ref):
    devices, _, groups, rows, lanes = in_ref.shape
    some = devices // RADIX
    size = some * rows
    few = size // GROUP

    def turn(re, im, j, sign):
        cos, sin = (
            jnp.broadcast_to(
                ref[j * few : (j + 1) * few][:, None, :], (few, GROUP, lanes)
            ).reshape(size, lanes)
            for ref in (cos_ref, sin_ref)
        )
        if sign > 0:
            return re * cos - im * sin, re * sin + im * cos
        return re * cos + im * sin, im * cos - re * sin

    def outer(group):
        blocks = []
        for q in range(RADIX):
            pair = [
                in_ref[q * some : (q + 1) * some, array, group].reshape(size, lanes)
                for array in range(2)
            ]
            blocks.append(jnp.concatenate(pair, axis=1).astype(jnp.float32))
        return [
            outer_dot(fo_ref[j], jnp.concatenate([re, im], axis=0))
            for j, (re, im) in enumerate(quarters(*blocks))
        ]

    def spectra(outers):
        turned = []
        for j, part in enumerate(outers):
            turned.append(
                [
                    jnp.concatenate(
                        turn(part[:size, at : at + lanes], part[size:, at : at + lanes], j, -1), axis=1
                    ).astype(jnp.bfloat16)
                    for at in (0, lanes)
                ]
            )
        return [dot(jnp.concatenate(part, axis=0), fi_ref[...]) for part in zip(*turned)]

    def product(sig, fil):
        sig_re, sig_im = sig[:, :lanes], sig[:, lanes:]
        fil_re, fil_im = fil[:, :lanes], fil[:, lanes:]
        prod = jnp.concatenate(
            [sig_re * fil_re - sig_im * fil_im, sig_re * fil_im + sig_im * fil_re], axis=1
        )
        return dot(prod.astype(jnp.bfloat16), ii_ref[...])

    def unturned(spread):
        results = []
        for j in range(RADIX):
            back = spread[j * size : (j + 1) * size]
            back = turn(back[:, :lanes], back[:, lanes:], j, 1)
            results.append(jnp.concatenate(back, axis=0).astype(jnp.bfloat16))
        return results

    def finish(group, first, second):
        parts = []
        for j, pair in enumerate(zip(first, second)):
            part = dot(io_ref[j], jnp.concatenate(pair, axis=1))
            parts.append((part[:size], part[size:]))
        for q, conv in enumerate(recombined(parts)):
            conv = conv.astype(jnp.bfloat16)
            for half in range(2):
                out_ref[q * some : (q + 1) * some, group + half] = conv[
                    :, half * lanes : (half + 1) * lanes
                ].reshape(some, rows, lanes)

    outers = [outer(group) for group in range(groups)]
    specs = [spectra(part) for part in outers]
    spreads = [product(*spec) for spec in specs]
    results = [unturned(spread) for spread in spreads]
    for group in range(0, groups, 2):
        finish(group, results[group], results[group + 1])


def token_sums(terms):
    tokens, channels = terms.shape
    part = terms[:, :LANES]
    for start in range(LANES, channels, LANES):
        part = part + terms[:, start : start + LANES]
    return part


def finish_kernel(conv_ref, sig_ref, gate_ref, skip_ref, sq_ref, out_ref, sums_ref):
    devices, groups, rows, lanes = conv_ref.shape
    parts = rows // GROUP
    span, channels = out_ref.shape
    width, some = channels // TILES, devices // TILES
    sums = None
    for tile in range(TILES):
        turned = conv_ref[tile * some : (tile + 1) * some].astype(jnp.float32)
        turned = turned.reshape(some * groups, rows, lanes)
        conv = jnp.concatenate(
            [
                turned[:, part * GROUP : (part + 1) * GROUP].reshape(width, lanes).T
                for part in range(parts)
            ],
            axis=0,
        )
        at = slice(tile * width, (tile + 1) * width)
        sig = sig_ref[:, at].astype(jnp.float32)
        mixed = gate_ref[:, at].astype(jnp.float32) * (conv + skip_ref[:, at] * sig)
        out_ref[:, at] = mixed.astype(jnp.bfloat16)
        terms = [token_sums(sig * mixed), token_sums(mixed * mixed)]
        sums = terms if sums is None else [a + b for a, b in zip(sums, terms)]
    for row, total in enumerate(sums):
        sums_ref[row : row + 1] = jnp.sum(total.T, axis=0, keepdims=True)
    sums_ref[2:3] = sq_ref[...]


def deliver_kernel(in_ref, out_ref, sem_ref):
    span = in_ref.shape[0] // TILES
    copies = [
        pltpu.make_async_copy(
            in_ref.at[pl.ds(tile * span, span)], out_ref.at[pl.ds(tile * span, span)], sem_ref.at[tile]
        )
        for tile in range(TILES)
    ]
    for copy in copies:
        copy.start()
    for copy in copies:
        copy.wait()


def call(kernel, out_shape, **kwargs):
    return pl.pallas_call(
        kernel,
        out_shape=out_shape,
        compiler_params=pltpu.CompilerParams(vmem_limit_bytes=VMEM_LIMIT),
        **kwargs,
    )


def local(signal, gating, filters, skip_gain):
    count = lax.axis_size("ctx")
    span, channels = signal.shape
    width = channels // count
    parts = span // LANES
    packed_tail = (width // GROUP, parts * GROUP, LANES)
    bf16, f32 = jnp.bfloat16, jnp.float32
    hbm = pl.BlockSpec(memory_space=pltpu.HBM)
    vmem = pl.BlockSpec(memory_space=pltpu.VMEM)
    tile_sems = pltpu.SemaphoreType.DMA((TILES,))
    packed, sig_sq = call(
        prepare_kernel,
        (
            jax.ShapeDtypeStruct((count, 2) + packed_tail, bf16),
            jax.ShapeDtypeStruct((1, span), f32),
        ),
        in_specs=[vmem, vmem],
        out_specs=(vmem, vmem),
    )(signal, filters.astype(bf16))
    chans, sections = lax.axis_size("chan"), lax.axis_size("section")
    last = sections - 1

    def total_first(part):
        total = part
        for hop in range(1, chans):
            total = total + lax.ppermute(
                part,
                ("chan", "section"),
                [(i * sections + last, (i + hop) % chans * sections + last) for i in range(chans)],
            )
        return total

    is_last = lax.axis_index("section") == last
    sig_sq = lax.cond(is_last, total_first, lambda part: part, sig_sq)
    packed, sig_sq = lax.optimization_barrier((packed, sig_sq))
    received = lax.all_to_all(packed, "ctx", split_axis=0, concat_axis=0, tiled=True)
    conv = call(conv_kernel, jax.ShapeDtypeStruct((count,) + packed_tail, bf16))(
        received, *conv_tables(count * parts, LANES)
    )
    returned = lax.all_to_all(conv, "ctx", split_axis=0, concat_axis=0, tiled=True)
    mixed, sums = call(
        finish_kernel,
        (jax.ShapeDtypeStruct((span, channels), bf16), jax.ShapeDtypeStruct((3, span), f32)),
        in_specs=[vmem] * 5,
        out_specs=(vmem, vmem),
    )(returned, signal, gating, skip_gain.reshape(1, channels), sig_sq)
    result = call(
        deliver_kernel,
        jax.ShapeDtypeStruct((span, channels), bf16),
        in_specs=[pl.BlockSpec(memory_space=pl.ANY)],
        out_specs=hbm,
        scratch_shapes=[tile_sems],
    )(mixed)
    reach = 2
    while reach <= chans:
        sums = sums + lax.ppermute(sums, "chan", [(i, i ^ (reach - 1)) for i in range(chans)])
        reach *= 2
    inner_total, out_total, sig_total = sums
    sig_total = jnp.where(is_last, sig_sq[0], sig_total)
    cosine = inner_total / jnp.sqrt((sig_total + EPSILON) * (out_total + EPSILON))
    return (result, cosine)


def solution(mesh):
    return jax.shard_map(
        local,
        mesh=mesh,
        in_specs=(
            P(("section", "ctx"), "chan"),
            P(("section", "ctx"), "chan"),
            P(("section", "ctx"), "chan"),
            P(("section", "chan")),
        ),
        out_specs=(P(("section", "ctx"), "chan"), P(("section", "ctx"))),
        check_vma=False,
    )
```
